256 devices in a mesh: ctx: 16 (over z_hi, x, core), tp: 16 (over y, z_lo).
Axes of the slice: x: 4, y: 4, z: 8 (z_hi: 2, z_lo: 4; z = z_hi * 4 + z_lo), core: 2. Of those that a mesh axis runs over, the one named last changes fastest.
Arguments:
- hidden: bfloat16 [8192, 8192], P('ctx'), may hold values from -8 to 8
- norm_gain: bfloat16 [8192], replicated, may hold values from 0.099609375 to 1.8984375
- trainer_query: bfloat16 [16, 8192, 256], P('tp', 'ctx'), may hold values from -1 to 1
- trainer_query_bias: bfloat16 [16, 256], P('tp'), may hold values from -3 to 3
- trainer_kv: bfloat16 [4, 8192, 256], P(None, 'ctx'), may hold values from -1 to 1
- trainer_kv_bias: bfloat16 [4, 256], replicated, may hold values from -3 to 3
- matching: int32 [16], replicated, may hold values from 0 to 15, as said below
- block_lists: int32 [32, 17], P('ctx'), may hold values from -1 to 31, as said below
- completion_lengths: int32 [16], replicated, may hold values from 1 to 256, as said below
Outputs:
- attended: bfloat16 [8192, 4096], P('ctx', 'tp')
The draws below stay inside these ranges and needn't reach their ends.
Inputs may be any that keep to these rules, and one draw needn't show every extreme that they name: `matching`: each number of 0 to 15 once. `block_lists`: row b < 16 lists blocks 0 to b; row 16 + c lists prefix blocks 0 to k - 1 for some k of 1 to 16, then block 16 + c; entries rise, the rest is -1; some row has 17 entries. `completion_lengths`: some completion has 256 live tokens.
All inputs are finite; a program needn't handle non-finite values.
Results may differ from the reference program's by a relative error of at most 0.0087.
Values may be sent and summed in bfloat16 or wider, within the bound.
No kernel may reach another device: no remote copies, remote signals or barrier semaphores. Data moves between devices by JAX's collectives and lax.ppermute only.
A program may use at most 64 MiB of HBM per device.

```python
import jax
import jax.numpy as jnp
from jax import lax

D = 8192
HD = 128
QHEADS = 32
KVHEADS = 4
BLK = 256
QCOLS = 256
SEQ = 8192
NBLK = 32
PBLK = 16
NCOMP = 16
MAXL = 17
N_TP = 16


def force_target(order, source, target):
    holder = jnp.argmax((order == target).astype(jnp.int32)).astype(jnp.int32)
    current = order[source]
    order = order.at[holder].set(current)
    return order.at[source].set(target)


def draw_matching(key, part):
    key = jax.random.fold_in(key, 8)
    order = jax.random.permutation(key, N_TP).astype(jnp.int32)
    root = jax.random.randint(jax.random.fold_in(key, 9), (), 0, N_TP).astype(jnp.int32)
    order = force_target(order, root, (root + N_TP // 2) % N_TP)
    order = force_target(order, (root + 1) % N_TP, (root + 2) % N_TP)
    order = force_target(order, (root + N_TP - 1) % N_TP, (root + N_TP - 2) % N_TP)
    return order.astype(jnp.int32)


def draw_hidden(key, part):
    key = jax.random.fold_in(key, 1)
    values = jax.random.normal(key, (SEQ, D), jnp.float32)
    return jnp.clip(values, -8.0, 8.0).astype(jnp.bfloat16)


def draw_trainer_query(key, part):
    key = jax.random.fold_in(key, 2)
    noise = jax.random.normal(key, (N_TP, D, QCOLS), jnp.float32) * D ** (-0.5)
    values = 1.7 * noise
    return jnp.clip(values, -1.0, 1.0).astype(jnp.bfloat16)


def draw_trainer_kv(key, part):
    key = jax.random.fold_in(key, 3)
    noise = jax.random.normal(key, (KVHEADS, D, 2 * HD), jnp.float32) * D ** (-0.5)
    key_part = 1.7 * noise[:, :, :HD]
    values = jnp.concatenate([key_part, noise[:, :, HD:]], axis=2)
    return jnp.clip(values, -1.0, 1.0).astype(jnp.bfloat16)


def draw_block_lists(key, part):
    key = jax.random.fold_in(key, 4)
    branch = jax.random.randint(key, (NCOMP,), 1, PBLK + 1)
    chosen = jax.random.randint(jax.random.fold_in(key, 5), (), 0, NCOMP)
    branch = jnp.where(jnp.arange(NCOMP) == chosen, PBLK, branch)
    column = jnp.arange(MAXL, dtype=jnp.int32)
    prefix_rows = jnp.where(column[None, :] <= jnp.arange(PBLK, dtype=jnp.int32)[:, None], column[None, :], -1)
    own = PBLK + jnp.arange(NCOMP, dtype=jnp.int32)
    completion_rows = jnp.where(column[None, :] < branch[:, None], column[None, :], jnp.where(column[None, :] == branch[:, None], own[:, None], -1))
    return jnp.concatenate([prefix_rows, completion_rows], axis=0).astype(jnp.int32)


def draw_completion_lengths(key, part):
    key = jax.random.fold_in(key, 6)
    lengths = jax.random.randint(key, (NCOMP,), 1, BLK + 1)
    chosen = jax.random.randint(jax.random.fold_in(key, 7), (), 0, NCOMP)
    return jnp.where(jnp.arange(NCOMP) == chosen, BLK, lengths).astype(jnp.int32)


def levels(own_key, shape, cuts, least, largest):
    gain, own = 1.0, jax.random.fold_in(own_key, 6)
    for dim, parts in cuts:
        steps = jnp.exp(jax.random.uniform(jax.random.fold_in(own, dim), (parts,), jnp.float32, least / len(cuts), largest / len(cuts)))
        gain = gain * jnp.repeat(steps, shape[dim] // parts).reshape([-1 if axis == dim else 1 for axis in range(len(shape))])
    return gain


def bell_draw(stream_key, extent, deviation, bound, cuts=(), kind=jnp.bfloat16):
    level = levels(stream_key, extent, cuts, -0.22, 0.18) if cuts else 1.0
    array = jax.random.normal(stream_key, extent, jnp.float32) * deviation * level
    return jnp.minimum(jnp.maximum(array, -bound), bound).astype(kind)


def setup_inputs(seed: int = 0) -> dict:
    streams_of = jax.random.split(jax.random.key(seed), 10)
    return {
        "hidden": draw_hidden(jax.random.fold_in(streams_of[9], 71), 0),
        "norm_gain": jnp.clip(1.0 + 0.18 * jax.random.normal(streams_of[1], (D,), jnp.float32), 0.099609375, 1.8984375).astype(jnp.bfloat16),
        "trainer_query": draw_trainer_query(jax.random.fold_in(streams_of[9], 71), 0),
        "trainer_query_bias": bell_draw(streams_of[3], (N_TP, QCOLS), 0.5, 3.0, ((0, 16),)),
        "trainer_kv": draw_trainer_kv(jax.random.fold_in(streams_of[9], 71), 0),
        "trainer_kv_bias": bell_draw(streams_of[5], (KVHEADS, 2 * HD), 0.5, 3.0),
        "matching": draw_matching(jax.random.fold_in(streams_of[9], 71), 0),
        "block_lists": draw_block_lists(jax.random.fold_in(streams_of[9], 71), 0),
        "completion_lengths": draw_completion_lengths(jax.random.fold_in(streams_of[9], 71), 0),
    }


THETA = 1000000.0
EPSILON = 1e-06

def rotary(vectors, positions):
    half = vectors.shape[-1] // 2
    freqs = THETA ** (-2.0 * jnp.arange(half, dtype=jnp.float32) / vectors.shape[-1])
    angles = positions.astype(jnp.float32)[:, None] * freqs[None, :]
    cosine = jnp.cos(angles)
    sine = jnp.sin(angles)
    first = vectors[..., :half]
    second = vectors[..., half:]
    return jnp.concatenate([first * cosine - second * sine, second * cosine + first * sine], axis=-1)

def reference(hidden, norm_gain, trainer_query, trainer_query_bias, trainer_kv, trainer_kv_bias, matching, block_lists, completion_lengths):
    total = hidden.shape[0]
    wide = hidden.astype(jnp.float32)
    squares = lax.optimization_barrier(jnp.mean(wide * wide, axis=1, keepdims=True))
    normed = (wide * lax.rsqrt(squares + EPSILON) * norm_gain.astype(jnp.float32)).astype(jnp.bfloat16)
    inverse = jnp.zeros((N_TP,), jnp.int32).at[matching].set(jnp.arange(N_TP, dtype=jnp.int32))
    query_weight = jnp.transpose(trainer_query[inverse], (1, 0, 2)).reshape(D, QHEADS * HD)
    query_bias = trainer_query_bias[inverse].reshape(QHEADS * HD)
    token_index = jnp.arange(total, dtype=jnp.int32)
    token_block = token_index // BLK
    counts = lax.optimization_barrier(jnp.sum((block_lists >= 0).astype(jnp.int32), axis=1))
    positions = jnp.where(token_block < PBLK, token_index, (counts[token_block] - 1) * BLK + token_index % BLK)
    projected = jnp.dot(normed, query_weight, preferred_element_type=jnp.float32) + query_bias.astype(jnp.float32)
    queries = rotary(jnp.transpose(projected.reshape(total, QHEADS, HD), (1, 0, 2)), positions).astype(jnp.bfloat16)
    kv_weight = jnp.transpose(trainer_kv, (1, 0, 2)).reshape(D, KVHEADS * 2 * HD)
    kv_all = jnp.dot(normed, kv_weight, preferred_element_type=jnp.float32) + trainer_kv_bias.reshape(KVHEADS * 2 * HD).astype(jnp.float32)
    kv_all = jnp.transpose(kv_all.reshape(total, KVHEADS, 2 * HD), (1, 0, 2))
    keys = rotary(kv_all[:, :, :HD], positions).astype(jnp.bfloat16)
    values = kv_all[:, :, HD:].astype(jnp.bfloat16)
    slot = jnp.clip(token_block - PBLK, 0, NCOMP - 1)
    live = (token_block < PBLK) | (token_index % BLK < completion_lengths[slot])
    allowed_blocks = jnp.any(block_lists[:, :, None] == jnp.arange(NBLK, dtype=jnp.int32)[None, None, :], axis=1)
    group = QHEADS // KVHEADS
    rows = min(512, total)
    turns = total // rows
    scale = HD ** (-0.5)

    def one_block(item):
        item = item.astype(jnp.int32)
        head_group = (item // turns).astype(jnp.int32)
        start = (item % turns * rows).astype(jnp.int32)
        zero = jnp.zeros((), jnp.int32)
        query = lax.dynamic_slice(queries, ((head_group * group).astype(jnp.int32), start, zero), (group, rows, HD)).astype(jnp.float32)
        key = lax.dynamic_index_in_dim(keys, head_group, 0, keepdims=False).astype(jnp.float32)
        value = lax.dynamic_index_in_dim(values, head_group, 0, keepdims=False).astype(jnp.float32)
        query_index = start + jnp.arange(rows, dtype=jnp.int32)
        mask = allowed_blocks[query_index // BLK][:, token_block] & live[None, :] & (token_index[None, :] <= query_index[:, None])
        scores = jnp.einsum('hqd,kd->hqk', query, key) * scale
        scores = jnp.where(mask[None], scores, -1e+30)
        top = lax.optimization_barrier(jnp.max(scores, axis=-1, keepdims=True))
        weights = jnp.where(mask[None], jnp.exp(scores - top), 0.0)
        weight_sum = lax.optimization_barrier(jnp.sum(weights, axis=-1, keepdims=True))
        rounded = lax.optimization_barrier(weights.astype(jnp.bfloat16)).astype(jnp.float32)
        mixed = jnp.einsum('hqk,kd->hqd', rounded, value)
        return (mixed / weight_sum).astype(jnp.bfloat16)
    blocks = lax.map(one_block, jnp.arange(KVHEADS * turns, dtype=jnp.int32))
    blocks = blocks.reshape(KVHEADS, turns, group, rows, HD)
    return jnp.transpose(blocks, (1, 3, 0, 2, 4)).reshape(total, QHEADS * HD)
```

```python
import functools
import math

import jax
import jax.numpy as jnp
from jax import lax
from jax.experimental import pallas as pl
from jax.experimental.pallas import tpu as pltpu
from jax.sharding import Mesh, PartitionSpec as P

BLK = 256
THETA = 1000000.0
EPSILON = 1e-06
BF = jnp.bfloat16
F32 = jnp.float32
ZH, X, CORE, Y, ZL = "zh", "x", "core", "y", "zl"
VMEM_LIMIT = 48 * 1024 * 1024


def full(shape):
    zeros = (0,) * len(shape)
    return pl.BlockSpec(shape, lambda *_: zeros)


def norm_kernel(order, h_ref, g_ref, o_ref):
    parts = o_ref.shape[0]
    width = o_ref.shape[2]
    total = None
    for k in range(parts):
        piece = h_ref[:, k * width : (k + 1) * width].astype(F32)
        square = piece * piece
        total = square if total is None else total + square
    mean = jnp.sum(total, axis=1, keepdims=True) * (1.0 / (parts * width))
    rs = lax.rsqrt(mean + EPSILON)
    for k in range(parts):
        off = pl.multiple_of(order[k] * width, width)
        piece = h_ref[:, pl.ds(off, width)].astype(F32)
        gain = g_ref[:, pl.ds(off, width)].astype(F32)
        o_ref[k] = (piece * rs * gain).astype(BF)


def norm(hidden, gain, order):
    rows, d = hidden.shape
    parts = 16
    width = d // parts
    step = 64
    return pl.pallas_call(
        norm_kernel,
        grid_spec=pltpu.PrefetchScalarGridSpec(
            num_scalar_prefetch=1,
            grid=(rows // step,),
            in_specs=[
                pl.BlockSpec((step, d), lambda i, o: (i, 0)),
                pl.BlockSpec((1, d), lambda i, o: (0, 0)),
            ],
            out_specs=pl.BlockSpec((parts, step, width), lambda i, o: (0, i, 0)),
        ),
        out_shape=jax.ShapeDtypeStruct((parts, rows, width), BF),
        compiler_params=pltpu.CompilerParams(vmem_limit_bytes=VMEM_LIMIT),
        cost_estimate=pl.CostEstimate(flops=rows * d * 8, bytes_accessed=4 * rows * d, transcendentals=0),
        name="norm",
    )(order, hidden, gain.reshape(1, d))


def kv_kernel(n_ref, *refs):
    w_refs = refs[:8]
    bias_ref, cos_ref, sin_ref, o_ref, left, right = refs[8:]
    k = pl.program_id(0)

    @pl.when(k == 0)
    def _():
        left[...] = jnp.zeros_like(left)
        right[...] = jnp.zeros_like(right)

    for i in range(16):

        @pl.when(k == i)
        def _():
            w = w_refs[i // 2][(i % 2) * 256 : (i % 2) * 256 + 256, :]
            left[...] += jnp.dot(n_ref[0, :, :256], w, preferred_element_type=F32)
            right[...] += jnp.dot(n_ref[0, :, 256:], w, preferred_element_type=F32)

    @pl.when(k == 15)
    def _():
        lt = left[...].T
        rt = right[...].T
        kv = lt[:64] + rt[64:] + bias_ref[:, :1]
        first, second = kv[:16], kv[16:32]
        cos, sin = cos_ref[...], sin_ref[...]
        o_ref[0:16] = (first * cos - second * sin).astype(BF)
        o_ref[16:32] = (second * cos + first * sin).astype(BF)
        o_ref[32:64] = kv[32:64].astype(BF)


def kv_project(normed, pieces, bias, cos, sin):
    parts, rows, width = normed.shape
    return pl.pallas_call(
        kv_kernel,
        grid=(parts,),
        in_specs=[pl.BlockSpec((1, rows, width), lambda k: (k, 0, 0))]
        + [full(p.shape) for p in pieces]
        + [full(bias.shape), full(cos.shape), full(sin.shape)],
        out_specs=full((64, rows)),
        out_shape=jax.ShapeDtypeStruct((64, rows), BF),
        scratch_shapes=[pltpu.VMEM((rows, 128), F32), pltpu.VMEM((rows, 128), F32)],
        compiler_params=pltpu.CompilerParams(vmem_limit_bytes=VMEM_LIMIT),
        cost_estimate=pl.CostEstimate(
            flops=2 * rows * parts * width * 256, bytes_accessed=2 * rows * parts * width + (1 << 20), transcendentals=0
        ),
        name="kv_project",
    )(normed, *pieces, bias, cos, sin)


def q_kernel(order, n_ref, *refs):
    w_refs = refs[:16]
    bias_ref, cos_ref, sin_ref, o_ref, acc, turned = refs[16:]
    k = pl.program_id(0)

    @pl.when(k == 0)
    def _():
        acc[...] = jnp.zeros_like(acc)

    for i in range(16):

        @pl.when(k == i)
        def _():
            acc[...] += jnp.dot(n_ref[0], w_refs[i][...], preferred_element_type=F32)

    @pl.when(k == 15)
    def _():
        cos, sin = cos_ref[...], sin_ref[...]
        for h in range(2):
            u = acc[:, h * 128 : (h + 1) * 128] + bias_ref[:, h * 128 : (h + 1) * 128]
            turned[:, h * 128 : (h + 1) * 128] = (u * cos + pltpu.roll(u, 64, 1) * sin).astype(BF)
        for d in range(4):
            off = pl.multiple_of(order[d] * 128, 128)
            o_ref[d] = turned[pl.ds(off, 128), :]


def q_project(normed, pieces, bias, cos, sin, order):
    parts, rows, width = normed.shape
    return pl.pallas_call(
        q_kernel,
        grid_spec=pltpu.PrefetchScalarGridSpec(
            num_scalar_prefetch=1,
            grid=(parts,),
            in_specs=[pl.BlockSpec((1, rows, width), lambda k, o: (k, 0, 0))]
            + [full(p.shape) for p in pieces]
            + [full(bias.shape), full(cos.shape), full(sin.shape)],
            out_specs=full((4, rows // 4, 256)),
            scratch_shapes=[pltpu.VMEM((rows, 256), F32), pltpu.VMEM((rows, 256), BF)],
        ),
        out_shape=jax.ShapeDtypeStruct((4, rows // 4, 256), BF),
        compiler_params=pltpu.CompilerParams(vmem_limit_bytes=VMEM_LIMIT),
        cost_estimate=pl.CostEstimate(
            flops=2 * rows * parts * width * 256, bytes_accessed=2 * rows * parts * width + (4 << 20), transcendentals=0
        ),
        name="q_project",
    )(order, normed, *pieces, bias, cos, sin)


def choose_kernel(row_tab, col_tab, *refs):
    o_ref = refs[4]
    f = pl.program_id(0)
    for e in range(4):

        @pl.when(row_tab[f] == e)
        def _():
            o_ref[...] = refs[e][...]


def choose(gathered, row_tab, col_tab):
    shape = gathered[0].shape
    block = (1,) + shape[1:]
    return pl.pallas_call(
        choose_kernel,
        grid_spec=pltpu.PrefetchScalarGridSpec(
            num_scalar_prefetch=2,
            grid=(4,),
            in_specs=[pl.BlockSpec(block, lambda f, r, c: (c[f], 0, 0)) for _ in gathered],
            out_specs=pl.BlockSpec(block, lambda f, r, c: (f, 0, 0)),
        ),
        out_shape=jax.ShapeDtypeStruct(shape, BF),
        compiler_params=pltpu.CompilerParams(vmem_limit_bytes=VMEM_LIMIT),
        cost_estimate=pl.CostEstimate(flops=0, bytes_accessed=5 << 18, transcendentals=0),
        name="choose",
    )(row_tab, col_tab, *gathered)


def attention_kernel(tab, *refs):
    q_refs = refs[:4]
    base_refs = refs[4:12]
    own_refs = refs[12:16]
    o_ref, kt, vt, qs = refs[16:]
    prefix = 4096

    def place(ref_piece, j, col):
        krow = pl.multiple_of(j * 16, 16)
        vrow = pl.multiple_of(j * 32, 32)
        kt[pl.ds(krow, 16), pl.ds(col, 512)] = ref_piece[0:16, :]
        kt[pl.ds(krow + 64, 16), pl.ds(col, 512)] = ref_piece[16:32, :]
        vt[pl.ds(vrow, 32), pl.ds(col, 512)] = ref_piece[32:64, :]

    for a in range(8):
        col = pl.multiple_of(tab[8 + a] * 512, 512)
        for d in range(4):
            place(base_refs[a].at[d], tab[16 + d], col)

    @pl.when(tab[24] == 0)
    def _():
        for d in range(4):
            place(base_refs[0].at[d], tab[16 + d], prefix)

    @pl.when(tab[24] != 0)
    def _():
        for d in range(4):
            place(own_refs[d], tab[20 + d], prefix)

    for f in range(4):
        where = tab[20 + f]
        blk = where // 2
        off = pl.multiple_of(lax.rem(where, 2) * 128, 128)
        for h in range(2):
            qs[blk, pl.ds(h * 256 + off, 128), :] = q_refs[f][:, h * 128 : (h + 1) * 128]

    factor = (128 ** -0.5) * math.log2(math.e)

    def lanes(p):
        total = p[:, :128]
        for i in range(1, p.shape[1] // 128):
            total = total + p[:, i * 128 : (i + 1) * 128]
        return total

    def pv(p, v):
        return lax.dot_general(p.astype(BF), v, (((1,), (1,)), ((), ())), preferred_element_type=F32)

    for blk in range(2):
        nfull = tab[blk]
        live = tab[2 + blk]
        q = qs[blk]
        c0 = prefix + blk * 256
        s = jnp.dot(q, kt[:, c0 : c0 + 256], preferred_element_type=F32) * factor
        row = lax.broadcasted_iota(jnp.int32, (512, 256), 0)
        row = jnp.where(row >= 256, row - 256, row)
        column = lax.broadcasted_iota(jnp.int32, (512, 256), 1)
        mask = (column <= row) & (column < live)
        s = jnp.where(mask, s, -1e30)
        top = jnp.max(s, axis=1, keepdims=True)
        p = jnp.where(mask, jnp.exp2(s - top), 0.0)
        state = (top, lanes(p), pv(p, vt[:, c0 : c0 + 256]))

        def step(begin, width, state):
            top, total, acc = state
            begin = pl.multiple_of(begin, 256)
            s = jnp.dot(q, kt[:, pl.ds(begin, width)], preferred_element_type=F32) * factor
            new = jnp.maximum(top, jnp.max(s, axis=1, keepdims=True))
            p = jnp.exp2(s - new)
            decay = jnp.exp2(top - new)
            return (new, total * decay + lanes(p), acc * decay + pv(p, vt[:, pl.ds(begin, width)]))

        state = lax.fori_loop(0, nfull // 2, lambda i, st: step(i * 512, 512, st), state)
        state = lax.fori_loop(0, lax.rem(nfull, 2), lambda i, st: step((nfull - 1) * 256, 256, st), state)
        top, total, acc = state
        result = (acc / jnp.sum(total, axis=1, keepdims=True)).astype(BF)
        for h in range(2):
            o_ref[blk * 256 : (blk + 1) * 256, h * 128 : (h + 1) * 128] = result[h * 256 : (h + 1) * 256]


def attention(tab, q_pieces, base, own):
    inputs = [*q_pieces, *base, *own]
    return pl.pallas_call(
        attention_kernel,
        grid_spec=pltpu.PrefetchScalarGridSpec(
            num_scalar_prefetch=1,
            grid=(1,),
            in_specs=[full(a.shape) for a in inputs],
            out_specs=full((512, 256)),
            scratch_shapes=[
                pltpu.VMEM((128, 4096 + 512), BF),
                pltpu.VMEM((128, 4096 + 512), BF),
                pltpu.VMEM((2, 512, 128), BF),
            ],
        ),
        out_shape=jax.ShapeDtypeStruct((512, 256), BF),
        compiler_params=pltpu.CompilerParams(vmem_limit_bytes=VMEM_LIMIT),
        cost_estimate=pl.CostEstimate(flops=2 << 30, bytes_accessed=3 << 20, transcendentals=4 << 20),
        name="attention",
    )(tab, *inputs)


def shift(v, axis, by):
    n = lax.axis_size(axis)
    return lax.ppermute(v, axis, [(i, (i + by) % n) for i in range(n)])


def flip(v, axis, bits):
    n = lax.axis_size(axis)
    return lax.ppermute(v, axis, [(i, i ^ bits) for i in range(n)])


def local(
    hidden,
    norm_gain,
    trainer_query,
    trainer_query_bias,
    trainer_kv,
    trainer_kv_bias,
    matching,
    block_lists,
    completion_lengths,
):
    zh, x, core, y, zl = (lax.axis_index(a).astype(jnp.int32) for a in (ZH, X, CORE, Y, ZL))
    rows = hidden.shape[0]
    ctx = (zh * 4 + x) * 2 + core
    four = jnp.arange(4, dtype=jnp.int32)

    ks = jnp.arange(16, dtype=jnp.int32)
    order = ((zh ^ (ks % 2)) * 4 + (x - (ks // 2) % 4) % 4) * 2 + (core ^ (ks // 8))

    with jax.named_scope("kv_weights"):
        head = lax.dynamic_index_in_dim(trainer_kv, y, 0, keepdims=False)
        out_col = jnp.arange(128, dtype=jnp.int32) % 64
        wanted = jnp.where(
            out_col < 16,
            zl * 16 + out_col,
            jnp.where(out_col < 32, 64 + zl * 16 + out_col - 16, 128 + zl * 32 + out_col - 32),
        )
        side = jnp.arange(128, dtype=jnp.int32) // 64
        pick = jnp.arange(256, dtype=jnp.int32)[:, None] == wanted[None, :]
        pick_l = (pick & (side == 0)[None, :]).astype(BF)
        pick_r = (pick & (side == 1)[None, :]).astype(BF)
        packed = (
            jnp.dot(head[:256], pick_l, preferred_element_type=F32)
            + jnp.dot(head[256:], pick_r, preferred_element_type=F32)
        ).astype(BF)
        head_bias = lax.dynamic_index_in_dim(trainer_kv_bias, y, 0, keepdims=False).astype(F32)
        own_bias = jnp.sum(jnp.where(pick[:, :64], head_bias[:, None], 0.0), axis=0)
        own_bias = jnp.broadcast_to(own_bias[:, None], (64, 128))
        both = jnp.concatenate([packed, flip(packed, ZH, 1)], axis=0)
        kv_near = [both] + [shift(both, X, d) for d in (1, 2, 3)]
        kv_pieces = kv_near + [flip(p, CORE, 1) for p in kv_near]

    with jax.named_scope("q_weights"):
        s0 = trainer_query[0]
        z0 = flip(s0, ZH, 1)
        near = []
        for d in range(4):
            near += [s0 if d == 0 else shift(s0, X, d), z0 if d == 0 else shift(z0, X, d)]
        q_pieces = near + [flip(p, CORE, 1) for p in near]

    normed = norm(hidden, norm_gain, order)

    counts = jnp.sum((block_lists >= 0).astype(jnp.int32), axis=1)
    token = jnp.arange(rows, dtype=jnp.int32)
    positions = (jnp.where(token < BLK, counts[0], counts[1]) - 1) * BLK + token % BLK
    freqs = THETA ** (-2.0 * jnp.arange(64, dtype=F32) / 128)
    angles = positions.astype(F32)[:, None] * freqs[None, :]
    cosine, sine = jnp.cos(angles), jnp.sin(angles)
    cos2 = jnp.concatenate([cosine, cosine], axis=1)
    sin2 = jnp.concatenate([-sine, sine], axis=1)
    own_freqs = lax.dynamic_slice_in_dim(freqs, zl * 16, 16, 0)
    own_angles = own_freqs[:, None] * positions.astype(F32)[None, :]
    cos_t, sin_t = jnp.cos(own_angles), jnp.sin(own_angles)

    with jax.named_scope("kv_spread"):
        piece = kv_project(normed, kv_pieces, own_bias, cos_t, sin_t)
        over = lax.ppermute(piece, (ZH, ZL), [(i, 4 + (3 - i)) for i in range(4)])
        start = jnp.where(zh == 0, piece, over)
        base0 = jnp.stack([start] + [flip(start, ZL, d) for d in (1, 2, 3)])
        own = [piece] + [
            lax.ppermute(piece, (ZH, ZL), [(4 + i, 4 + (i ^ d)) for i in range(4)]) for d in (1, 2, 3)
        ]
        base_near = [base0] + [shift(base0, X, d) for d in (1, 2, 3)]
        base = base_near + [flip(p, CORE, 1) for p in base_near]

    with jax.named_scope("queries"):
        parts = q_project(
            normed, q_pieces, trainer_query_bias.astype(F32), cos2, sin2, zl ^ four
        )
        mine = jnp.stack([parts[0]] + [flip(parts[d], ZL, d) for d in (1, 2, 3)])
        gathered = [mine] + [flip(mine, Y, e) for e in (1, 2, 3)]
        target = y * 4 + (zl ^ four)
        source = jnp.sum(
            jnp.where(matching[None, :] == target[:, None], jnp.arange(16, dtype=jnp.int32)[None, :], 0), axis=1
        )
        chosen = choose(gathered, (source // 4) ^ y, (source % 4) ^ zl)
        final = [chosen[0]] + [flip(chosen[f], ZL, f) for f in (1, 2, 3)]

    blocks = ctx * 2 + jnp.arange(2, dtype=jnp.int32)
    slots = jnp.arange(16, dtype=jnp.int32)
    lengths = jnp.sum(
        jnp.where((blocks[:, None] - 16) == slots[None, :], completion_lengths[None, :], 0), axis=1
    )
    live = jnp.where(blocks < 16, BLK, lengths)
    tab = jnp.concatenate(
        [
            counts - 1,
            live,
            jnp.zeros((4,), jnp.int32),
            ((x - four) % 4) * 2 + core,
            ((x - four) % 4) * 2 + (core ^ 1),
            zl ^ four ^ (3 * zh),
            zl ^ four,
            zh[None],
        ]
    ).astype(jnp.int32)
    return attention(tab, final, base, own)


def solution(mesh):
    fine = Mesh(mesh.devices.reshape(2, 4, 2, 4, 4), (ZH, X, CORE, Y, ZL))
    ctx = (ZH, X, CORE)
    tp = (Y, ZL)
    in_specs = (
        P(ctx, None),
        P(),
        P(tp, ctx, None),
        P(tp, None),
        P(None, ctx, None),
        P(),
        P(),
        P(ctx, None),
        P(),
    )
    return jax.shard_map(local, mesh=fine, in_specs=in_specs, out_specs=P(ctx, tp), check_vma=False)
```

```python
import functools
import math

import jax
import jax.numpy as jnp
from jax import lax
from jax.experimental import pallas as pl
from jax.experimental.pallas import tpu as pltpu
from jax.sharding import Mesh, PartitionSpec as P

BLK = 256
THETA = 1000000.0
EPSILON = 1e-06
BF = jnp.bfloat16
F32 = jnp.float32
ZH, X, CORE, Y, ZL = "zh", "x", "core", "y", "zl"


def full(shape):
    zeros = (0,) * len(shape)
    return pl.BlockSpec(shape, lambda *_: zeros)


CHEAP = pl.CostEstimate(flops=0, bytes_accessed=0, transcendentals=0)
SIX_US = pl.CostEstimate(flops=0, bytes_accessed=20 << 20, transcendentals=0)
HBM = pl.BlockSpec(memory_space=pltpu.HBM)
VMEM_LIMIT = 40 << 20
VMEM_MOST = 60 << 20


THREE_US = pl.CostEstimate(flops=0, bytes_accessed=10 << 20, transcendentals=0)


def norm_kernel(order, h_ref, g_ref, near_ref, far_ref):
    parts, step, width = near_ref.shape

    def square(k, total):
        piece = h_ref[:, pl.ds(pl.multiple_of(k * width, width), width)].astype(F32)
        return total + piece * piece

    total = lax.fori_loop(0, 2 * parts, square, jnp.zeros((step, width), F32), unroll=4)
    mean = jnp.sum(total, axis=1, keepdims=True) * (1.0 / (2 * parts * width))
    rs = lax.rsqrt(mean + EPSILON)
    for half, o_ref in ((0, near_ref), (parts, far_ref)):

        def scale(k, carry):
            off = pl.multiple_of(order[half + k] * width, width)
            piece = h_ref[:, pl.ds(off, width)].astype(F32)
            gain = g_ref[:, pl.ds(off, width)].astype(F32)
            o_ref[k] = (piece * rs * gain).astype(BF)
            return carry

        lax.fori_loop(0, parts, scale, 0, unroll=4)


def norm(hidden, gain, order):
    rows, d = hidden.shape
    parts = 8
    width = d // parts // 2
    step = 64
    block = pl.BlockSpec((parts, step, width), lambda i, o: (0, i, 0))
    return pl.pallas_call(
        norm_kernel,
        grid_spec=pltpu.PrefetchScalarGridSpec(
            num_scalar_prefetch=1,
            grid=(rows // step,),
            in_specs=[
                pl.BlockSpec((step, d), lambda i, o: (i, 0)),
                pl.BlockSpec((1, d), lambda i, o: (0, 0)),
            ],
            out_specs=[block, block],
        ),
        out_shape=[jax.ShapeDtypeStruct((parts, rows, width), BF)] * 2,
        compiler_params=pltpu.CompilerParams(vmem_limit_bytes=VMEM_LIMIT),
        cost_estimate=SIX_US,
        name="norm",
    )(order, hidden, gain.reshape(1, d))


def fetch(n_refs, ks, nbuf, nsem, w_refs, wbuf, wsem):
    per = len(ks) // len(w_refs)
    for i, w_ref in enumerate(w_refs):
        pltpu.make_async_copy(w_ref, wbuf.at[i], wsem.at[i]).start()
        for j in range(i * per, (i + 1) * per):
            for t, n_ref in enumerate(n_refs):
                pltpu.make_async_copy(n_ref.at[ks[j]], nbuf.at[t, j], nsem.at[t, j]).start()


def kv_kernel(near_ref, far_ref, *refs):
    w_refs = refs[:4]
    own_ref, other_ref, nbuf, wbuf, left, right, nsem, wsem = refs[4:]
    fetch((near_ref, far_ref), (0, 4, 1, 5, 2, 6, 3, 7), nbuf, nsem, w_refs, wbuf, wsem)
    left[...] = jnp.zeros_like(left)
    right[...] = jnp.zeros_like(right)

    def step(i, carry):
        pltpu.make_async_copy(w_refs[0], wbuf.at[i], wsem.at[i]).wait()
        w0, w1 = wbuf[i, :256, :], wbuf[i, 256:, :]
        for t in range(2):
            for r in range(2):
                pltpu.make_async_copy(near_ref.at[0], nbuf.at[t, 2 * i + r], nsem.at[t, 2 * i + r]).wait()
            n0, n1 = nbuf.at[t, 2 * i], nbuf.at[t, 2 * i + 1]
            left[t] += jnp.dot(n0[:, :256], w0, preferred_element_type=F32) + jnp.dot(
                n1[:, :256], w1, preferred_element_type=F32
            )
            right[t] += jnp.dot(n0[:, 256:], w0, preferred_element_type=F32) + jnp.dot(
                n1[:, 256:], w1, preferred_element_type=F32
            )
        return carry

    lax.fori_loop(0, 4, step, 0)
    for t, o_ref in ((0, own_ref), (1, other_ref)):
        o_ref[...] = left[t].T[:64] + right[t].T[64:]


def kv_project(near, far, pieces):
    parts, rows, width = near.shape
    return pl.pallas_call(
        kv_kernel,
        in_specs=[HBM] * 6,
        out_specs=[full((64, rows))] * 2,
        out_shape=[jax.ShapeDtypeStruct((64, rows), F32)] * 2,
        scratch_shapes=[
            pltpu.VMEM((2, parts, rows, width), BF),
            pltpu.VMEM((4, 512, 128), BF),
            pltpu.VMEM((2, rows, 128), F32),
            pltpu.VMEM((2, rows, 128), F32),
            pltpu.SemaphoreType.DMA((2, 8)),
            pltpu.SemaphoreType.DMA((4,)),
        ],
        compiler_params=pltpu.CompilerParams(vmem_limit_bytes=VMEM_MOST),
        cost_estimate=SIX_US,
        name="kv_project",
    )(near, far, *pieces)


def kv_finish_kernel(one_ref, two_ref, bias_ref, cos_ref, sin_ref, o_ref):
    kv = one_ref[...] + two_ref[...] + bias_ref[:, :1]
    first, second = kv[:16], kv[16:32]
    cos, sin = cos_ref[...], sin_ref[...]
    o_ref[0:16] = (first * cos - second * sin).astype(BF)
    o_ref[16:32] = (second * cos + first * sin).astype(BF)
    o_ref[32:64] = kv[32:64].astype(BF)


def kv_finish(one, two, bias, cos, sin):
    inputs = [one, two, bias, cos, sin]
    return pl.pallas_call(
        kv_finish_kernel,
        in_specs=[full(v.shape) for v in inputs],
        out_specs=full(one.shape),
        out_shape=jax.ShapeDtypeStruct(one.shape, BF),
        compiler_params=pltpu.CompilerParams(vmem_limit_bytes=8 << 20),
        cost_estimate=CHEAP,
        name="kv_finish",
    )(*inputs)


def q_kernel(first, near_ref, far_ref, *refs):
    w_refs, refs = refs[:4], refs[4:]
    if first:
        so_far, refs = refs[:2], refs[2:]
    own_ref, other_ref, nbuf, wbuf, nsem, wsem = refs
    fetch((near_ref, far_ref), range(first, first + 4), nbuf, nsem, w_refs, wbuf, wsem)
    for t, o_ref in ((0, own_ref), (1, other_ref)):
        o_ref[...] = so_far[t][...] if first else jnp.zeros_like(o_ref)

    def step(i, carry):
        for r in range(2):
            pltpu.make_async_copy(w_refs[0], wbuf.at[2 * i + r], wsem.at[2 * i + r]).wait()
        for t, o_ref in ((0, own_ref), (1, other_ref)):
            out = None
            for r in range(2):
                k = 2 * i + r
                pltpu.make_async_copy(near_ref.at[0], nbuf.at[t, k], nsem.at[t, k]).wait()
                part = jnp.dot(nbuf[t, k], wbuf[k], preferred_element_type=F32)
                out = part if out is None else out + part
            o_ref[...] += out
        return carry

    lax.fori_loop(0, 2, step, 0)


def q_project(first, near, far, pieces, so_far):
    parts, rows, width = near.shape
    shape = jax.ShapeDtypeStruct((rows, 256), F32)
    return pl.pallas_call(
        functools.partial(q_kernel, first),
        in_specs=[HBM] * 6 + [full(shape.shape)] * len(so_far),
        out_specs=[full(shape.shape)] * 2,
        out_shape=[shape] * 2,
        scratch_shapes=[
            pltpu.VMEM((2, 4, rows, width), BF),
            pltpu.VMEM((4, 512, 256), BF),
            pltpu.SemaphoreType.DMA((2, 4)),
            pltpu.SemaphoreType.DMA((4,)),
        ],
        compiler_params=pltpu.CompilerParams(vmem_limit_bytes=VMEM_MOST),
        cost_estimate=THREE_US,
        name="q_project",
    )(near, far, *pieces, *so_far)


def choose_kernel(tab, *refs):
    sources, outs = refs[:4], refs[4:]
    for e in range(4):
        for d in range(4):

            @pl.when(tab[e] == d)
            def _():
                outs[e][...] = sources[d][...]


def choose(tab, sources):
    shape = sources[0].shape
    return pl.pallas_call(
        choose_kernel,
        grid_spec=pltpu.PrefetchScalarGridSpec(
            num_scalar_prefetch=1,
            grid=(1,),
            in_specs=[full(shape)] * 4,
            out_specs=[full(shape)] * 4,
        ),
        out_shape=[jax.ShapeDtypeStruct(shape, BF)] * 4,
        compiler_params=pltpu.CompilerParams(vmem_limit_bytes=8 << 20),
        cost_estimate=CHEAP,
        name="choose",
    )(tab, *sources)


def settle_kernel(tab, *refs):
    w_ref, bias_ref = refs[4:]
    for d in range(4):

        @pl.when(tab[0] == d)
        def _():
            w_ref[...] = refs[d][:512, :]
            bias_ref[...] = refs[d][512:, :].astype(F32)


def settle(tab, candidates):
    outs = [jax.ShapeDtypeStruct((512, 256), BF), jax.ShapeDtypeStruct((16, 256), F32)]
    return pl.pallas_call(
        settle_kernel,
        grid_spec=pltpu.PrefetchScalarGridSpec(
            num_scalar_prefetch=1,
            grid=(1,),
            in_specs=[full(candidates[0].shape)] * 4,
            out_specs=[full(o.shape) for o in outs],
        ),
        out_shape=outs,
        compiler_params=pltpu.CompilerParams(vmem_limit_bytes=8 << 20),
        cost_estimate=CHEAP,
        name="settle",
    )(tab, *candidates)


def place(ref_piece, j, kt, vt, col):
    krow = pl.multiple_of(j * 16, 16)
    vrow = pl.multiple_of(j * 32, 32)
    kt[pl.ds(krow, 16), pl.ds(col, 512)] = ref_piece[0:16, :]
    kt[pl.ds(krow + 64, 16), pl.ds(col, 512)] = ref_piece[16:32, :]
    vt[pl.ds(vrow, 32), pl.ds(col, 512)] = ref_piece[32:64, :]


def assemble_kernel(tab, *refs):
    o_ref = refs[4]
    for a in range(4):
        col = pl.multiple_of(tab[8 + a] * 512, 512)

        def one(d, carry):
            place(refs[a].at[d], tab[16 + d], o_ref.at[0], o_ref.at[1], col)
            return carry

        lax.fori_loop(0, 4, one, 0)


def assemble(tab, base):
    shape = jax.ShapeDtypeStruct((2, 128, 2048), BF)
    return pl.pallas_call(
        assemble_kernel,
        grid_spec=pltpu.PrefetchScalarGridSpec(
            num_scalar_prefetch=1,
            grid=(1,),
            in_specs=[full(a.shape) for a in base],
            out_specs=full(shape.shape),
        ),
        out_shape=shape,
        compiler_params=pltpu.CompilerParams(vmem_limit_bytes=8 << 20),
        cost_estimate=CHEAP,
        name="assemble",
    )(tab, *base)


def attention_kernel(
    tab, one_ref, two_ref, bias_ref, cos_ref, sin_ref, own_ref, near_ref, far_ref, o_ref, qs, kv, own_kt, own_vt, sems
):
    core = tab[24]
    copies = [
        pltpu.make_async_copy(ref, kv.at[place_at], sems.at[i])
        for i, (ref, place_at) in enumerate(((near_ref, core), (far_ref, 1 - core)))
    ]
    for copy in copies:
        copy.start()
    for d in range(4):
        place(own_ref.at[d], tab[20 + d], own_kt, own_vt, 0)
    for blk in range(2):
        rows = slice(blk * 256, (blk + 1) * 256)
        for h in range(2):
            cols = slice(h * 128, (h + 1) * 128)
            u = one_ref[rows, cols] + two_ref[rows, cols] + bias_ref[0:1, cols]
            turned = u * cos_ref[rows, :] + pltpu.roll(u, 64, 1) * sin_ref[rows, :]
            qs[blk, h * 256 : (h + 1) * 256, :] = turned.astype(BF)

    factor = (128 ** -0.5) * math.log2(math.e)

    def lanes(p):
        total = p[:, :128]
        for i in range(1, p.shape[1] // 128):
            total = total + p[:, i * 128 : (i + 1) * 128]
        return total

    def pv(p, v):
        return lax.dot_general(p.astype(BF), v, (((1,), (1,)), ((), ())), preferred_element_type=F32)

    def first(blk):
        live = tab[2 + blk]
        c0 = blk * 256
        s = jnp.dot(qs[blk], own_kt[:, c0 : c0 + 256], preferred_element_type=F32) * factor
        row = lax.broadcasted_iota(jnp.int32, (512, 256), 0)
        row = jnp.where(row >= 256, row - 256, row)
        column = lax.broadcasted_iota(jnp.int32, (512, 256), 1)
        mask = (column <= row) & (column < live)
        s = jnp.where(mask, s, -1e30)
        top = jnp.max(s, axis=1, keepdims=True)
        p = jnp.where(mask, jnp.exp2(s - top), 0.0)
        return (top, lanes(p), pv(p, own_vt[:, c0 : c0 + 256]))

    def step(blk, c, width, state):
        top, total, acc = state
        side = lax.rem(c, 2)
        keys = pl.ds(pl.multiple_of(c // 2 * 512, 512), width)
        s = jnp.dot(qs[blk], kv[side, 0, :, keys], preferred_element_type=F32) * factor
        new = jnp.maximum(top, jnp.max(s, axis=1, keepdims=True))
        p = jnp.exp2(s - new)
        decay = jnp.exp2(top - new)
        return (new, total * decay + lanes(p), acc * decay + pv(p, kv[side, 1, :, keys]))

    states = [first(0), first(1)]
    for copy in copies:
        copy.wait()
    for blk in range(2):
        n = tab[blk]
        state = lax.fori_loop(0, n // 2, lambda c, st: step(blk, c, 512, st), states[blk])
        state = lax.fori_loop(0, lax.rem(n, 2), lambda i, st: step(blk, n // 2, 256, st), state)
        top, total, acc = state
        result = (acc / jnp.sum(total, axis=1, keepdims=True)).astype(BF)
        for h in range(2):
            o_ref[blk * 256 : (blk + 1) * 256, h * 128 : (h + 1) * 128] = result[h * 256 : (h + 1) * 256]


def attention(tab, one, two, bias, cos, sin, own, near, far):
    inputs = [one, two, bias, cos, sin, own]
    return pl.pallas_call(
        attention_kernel,
        grid_spec=pltpu.PrefetchScalarGridSpec(
            num_scalar_prefetch=1,
            grid=(1,),
            in_specs=[full(a.shape) for a in inputs] + [HBM] * 2,
            out_specs=full((512, 256)),
            scratch_shapes=[
                pltpu.VMEM((2, 512, 128), BF),
                pltpu.VMEM((2, 2, 128, 2048), BF),
                pltpu.VMEM((128, 512), BF),
                pltpu.VMEM((128, 512), BF),
                pltpu.SemaphoreType.DMA((2,)),
            ],
        ),
        out_shape=jax.ShapeDtypeStruct((512, 256), BF),
        compiler_params=pltpu.CompilerParams(vmem_limit_bytes=VMEM_LIMIT),
        cost_estimate=CHEAP,
        name="attention",
    )(tab, *inputs, near, far)


def shift(v, axis, by):
    n = lax.axis_size(axis)
    return lax.ppermute(v, axis, [(i, (i + by) % n) for i in range(n)])


def flip(v, axis, bits):
    n = lax.axis_size(axis)
    return lax.ppermute(v, axis, [(i, i ^ bits) for i in range(n)])


def after(value, *others):
    return lax.optimization_barrier((value, *others))[0]


def each(fn, values, *others):
    return [fn(after(v, *others) if others else v) for v in values]


def local(
    hidden,
    norm_gain,
    trainer_query,
    trainer_query_bias,
    trainer_kv,
    trainer_kv_bias,
    matching,
    block_lists,
    completion_lengths,
):
    zh, x, core, y, zl = (lax.axis_index(a).astype(jnp.int32) for a in (ZH, X, CORE, Y, ZL))
    rows = hidden.shape[0]
    ctx = (zh * 4 + x) * 2 + core
    four = jnp.arange(4, dtype=jnp.int32)

    ks = jnp.arange(16, dtype=jnp.int32)
    order = ((zh ^ ((ks >> 2) & 1)) * 4 + (x ^ (ks & 3))) * 2 + (core ^ (ks >> 3))
    near, far_out = norm(hidden, norm_gain, order)

    head = lax.dynamic_index_in_dim(trainer_kv, y, 0, keepdims=False)
    out_col = jnp.arange(128, dtype=jnp.int32) % 64
    wanted = jnp.where(
        out_col < 16,
        zl * 16 + out_col,
        jnp.where(out_col < 32, 64 + zl * 16 + out_col - 16, 128 + zl * 32 + out_col - 32),
    )
    side = jnp.arange(128, dtype=jnp.int32) // 64
    pick = jnp.arange(256, dtype=jnp.int32)[:, None] == wanted[None, :]
    pick_l = (pick & (side == 0)[None, :]).astype(BF)
    pick_r = (pick & (side == 1)[None, :]).astype(BF)
    packed = (
        jnp.dot(head[:256], pick_l, preferred_element_type=F32)
        + jnp.dot(head[256:], pick_r, preferred_element_type=F32)
    ).astype(BF)
    head_bias = lax.dynamic_index_in_dim(trainer_kv_bias, y, 0, keepdims=False).astype(F32)
    own_bias = jnp.sum(jnp.where(pick[:, :64], head_bias[:, None], 0.0), axis=0)
    own_bias = jnp.broadcast_to(own_bias[:, None], (64, 128))

    source = lambda tz: jnp.sum(
        jnp.where(matching[None, :] == (y * 4 + tz)[:, None], jnp.arange(16, dtype=jnp.int32)[None, :], 0), axis=1
    )
    src = source(zl ^ four)
    bias_rows = jnp.broadcast_to(trainer_query_bias, (16, 256))
    block = jnp.concatenate([trainer_query[0], bias_rows], axis=0)
    gathered = [block] + [flip(block, Y, e) for e in (1, 2, 3)]
    both = jnp.concatenate([packed, flip(packed, ZH, 1)], axis=0)
    tab_1 = ((src // 4) ^ y).astype(jnp.int32)
    sent = choose(after(tab_1, near, both), gathered)
    both = after(both, sent[0])
    p_near = [both] + [flip(both, X, d) for d in (1, 2, 3)]
    far = flip(after(far_out, sent[0]), CORE, 1)
    candidates = [sent[0]] + [flip(sent[f], ZL, f) for f in (1, 2, 3)]

    counts = jnp.sum((block_lists >= 0).astype(jnp.int32), axis=1)
    token = jnp.arange(rows, dtype=jnp.int32)
    positions = (jnp.where(token < BLK, counts[0], counts[1]) - 1) * BLK + token % BLK
    freqs = THETA ** (-2.0 * jnp.arange(64, dtype=F32) / 128)
    angles = positions.astype(F32)[:, None] * freqs[None, :]
    cosine, sine = jnp.cos(angles), jnp.sin(angles)
    cos2 = jnp.concatenate([cosine, cosine], axis=1)
    sin2 = jnp.concatenate([-sine, sine], axis=1)
    own_freqs = lax.dynamic_slice_in_dim(freqs, zl * 16, 16, 0)
    own_angles = own_freqs[:, None] * positions.astype(F32)[None, :]
    cos_t, sin_t = jnp.cos(own_angles), jnp.sin(own_angles)

    tab_2 = ((src[:1] % 4) ^ zl).astype(jnp.int32)
    s0, bias = settle(after(tab_2, far, *p_near), candidates)
    z0 = flip(s0, ZH, 1)
    s_near = [s0] + [flip(s0, X, d) for d in (1, 2, 3)]

    kv_own, kv_other = kv_project(after(near, s0), far, p_near)
    kv_other, z0, *s_near = lax.optimization_barrier((kv_other, z0, *s_near))
    z_near = [z0] + [flip(z0, X, d) for d in (1, 2, 3)]
    piece = kv_finish(kv_own, flip(kv_other, CORE, 1), own_bias, cos_t, sin_t)
    over = lax.ppermute(piece, (ZH, ZL), [(i, 4 + (3 - i)) for i in range(4)])
    start = jnp.where(zh == 0, piece, over)
    pair = jnp.stack([start, piece])
    pairs = [pair] + [flip(pair, ZL, d) for d in (1, 2, 3)]
    base0 = jnp.stack([p[0] for p in pairs])
    own = jnp.stack([p[1] for p in pairs])
    q_half = list(q_project(0, near, far, s_near, []))
    base0, q_half[0], *z_near = lax.optimization_barrier((base0, q_half[0], *z_near))
    base_near = [base0] + [flip(base0, X, d) for d in (1, 2, 3)]
    q_own, q_other = q_project(4, near, far, z_near, q_half)
    q_two = flip(q_other, CORE, 1)
    base_near[0] = after(base_near[0], q_own)

    blocks = ctx * 2 + jnp.arange(2, dtype=jnp.int32)
    slots = jnp.arange(16, dtype=jnp.int32)
    lengths = jnp.sum(
        jnp.where((blocks[:, None] - 16) == slots[None, :], completion_lengths[None, :], 0), axis=1
    )
    live = jnp.where(blocks < 16, BLK, lengths)
    tab = jnp.concatenate(
        [
            counts - 1,
            live,
            jnp.zeros((4,), jnp.int32),
            x ^ four,
            jnp.zeros((4,), jnp.int32),
            zl ^ four ^ (3 * zh),
            zl ^ four,
            core[None],
        ]
    ).astype(jnp.int32)
    whole = assemble(tab, base_near)
    return attention(tab, q_own, q_two, bias, cos2, sin2, own, whole, flip(whole, CORE, 1))


def solution(mesh):
    fine = Mesh(mesh.devices.reshape(2, 4, 2, 4, 4), (ZH, X, CORE, Y, ZL))
    ctx = (ZH, X, CORE)
    tp = (Y, ZL)
    in_specs = (
        P(ctx, None),
        P(),
        P(tp, ctx, None),
        P(tp, None),
        P(None, ctx, None),
        P(),
        P(),
        P(ctx, None),
        P(),
    )
    return jax.shard_map(local, mesh=fine, in_specs=in_specs, out_specs=P(ctx, tp), check_vma=False)
```

```python
import functools
import math

import jax
import jax.numpy as jnp
from jax import lax
from jax.experimental import pallas as pl
from jax.experimental.pallas import tpu as pltpu
from jax.sharding import Mesh, PartitionSpec as P

BLK = 256
THETA = 1000000.0
EPSILON = 1e-06
BF = jnp.bfloat16
F32 = jnp.float32
ZH, X, CORE, Y, ZL = "zh", "x", "core", "y", "zl"


def full(shape):
    zeros = (0,) * len(shape)
    return pl.BlockSpec(shape, lambda *_: zeros)


CHEAP = pl.CostEstimate(flops=0, bytes_accessed=0, transcendentals=0)
SIX_US = pl.CostEstimate(flops=0, bytes_accessed=20 << 20, transcendentals=0)
HBM = pl.BlockSpec(memory_space=pltpu.HBM)
VMEM_LIMIT = 40 << 20
VMEM_MOST = 60 << 20


THREE_US = pl.CostEstimate(flops=0, bytes_accessed=10 << 20, transcendentals=0)


def norm_kernel(order, h_ref, g_ref, near_ref, far_ref):
    parts, step, width = near_ref.shape

    def square(k, total):
        piece = h_ref[:, pl.ds(pl.multiple_of(k * width, width), width)].astype(F32)
        return total + piece * piece

    total = lax.fori_loop(0, 2 * parts, square, jnp.zeros((step, width), F32), unroll=4)
    mean = jnp.sum(total, axis=1, keepdims=True) * (1.0 / (2 * parts * width))
    rs = lax.rsqrt(mean + EPSILON)
    for half, o_ref in ((0, near_ref), (parts, far_ref)):

        def scale(k, carry):
            off = pl.multiple_of(order[half + k] * width, width)
            piece = h_ref[:, pl.ds(off, width)].astype(F32)
            gain = g_ref[:, pl.ds(off, width)].astype(F32)
            o_ref[k] = (piece * rs * gain).astype(BF)
            return carry

        lax.fori_loop(0, parts, scale, 0, unroll=4)


def norm(hidden, gain, order):
    rows, d = hidden.shape
    parts = 8
    width = d // parts // 2
    step = 64
    block = pl.BlockSpec((parts, step, width), lambda i, o: (0, i, 0))
    return pl.pallas_call(
        norm_kernel,
        grid_spec=pltpu.PrefetchScalarGridSpec(
            num_scalar_prefetch=1,
            grid=(rows // step,),
            in_specs=[
                pl.BlockSpec((step, d), lambda i, o: (i, 0)),
                pl.BlockSpec((1, d), lambda i, o: (0, 0)),
            ],
            out_specs=[block, block],
        ),
        out_shape=[jax.ShapeDtypeStruct((parts, rows, width), BF)] * 2,
        compiler_params=pltpu.CompilerParams(vmem_limit_bytes=VMEM_LIMIT),
        cost_estimate=SIX_US,
        name="norm",
    )(order, hidden, gain.reshape(1, d))


def fetch(n_refs, ks, nbuf, nsem, w_refs, wbuf, wsem):
    per = len(ks) // len(w_refs)
    for i, w_ref in enumerate(w_refs):
        pltpu.make_async_copy(w_ref, wbuf.at[i], wsem.at[i]).start()
        for j in range(i * per, (i + 1) * per):
            for t, n_ref in enumerate(n_refs):
                pltpu.make_async_copy(n_ref.at[ks[j]], nbuf.at[t, j], nsem.at[t, j]).start()


def kv_kernel(near_ref, far_ref, *refs):
    w_refs = refs[:4]
    own_ref, other_ref, nbuf, wbuf, acc, nsem, wsem = refs[4:]
    fetch((near_ref, far_ref), (0, 4, 1, 5, 2, 6, 3, 7), nbuf, nsem, w_refs, wbuf, wsem)
    acc[...] = jnp.zeros_like(acc)

    def step(i, carry):
        pltpu.make_async_copy(w_refs[0], wbuf.at[i], wsem.at[i]).wait()
        for t in range(2):
            out = None
            for r in range(2):
                k = 2 * i + r
                pltpu.make_async_copy(near_ref.at[0], nbuf.at[t, k], nsem.at[t, k]).wait()
                part = jnp.dot(nbuf[t, k], wbuf[i, r], preferred_element_type=F32)
                out = part if out is None else out + part
            acc[t] += out
        return carry

    lax.fori_loop(0, 4, step, 0)
    for t, o_ref in ((0, own_ref), (1, other_ref)):
        o_ref[...] = acc[t].T


def kv_project(near, far, pieces):
    parts, rows, width = near.shape
    return pl.pallas_call(
        kv_kernel,
        in_specs=[HBM] * 6,
        out_specs=[full((128, rows))] * 2,
        out_shape=[jax.ShapeDtypeStruct((128, rows), F32)] * 2,
        scratch_shapes=[
            pltpu.VMEM((2, parts, rows, width), BF),
            pltpu.VMEM((4, 2, 512, 128), BF),
            pltpu.VMEM((2, rows, 128), F32),
            pltpu.SemaphoreType.DMA((2, 8)),
            pltpu.SemaphoreType.DMA((4,)),
        ],
        compiler_params=pltpu.CompilerParams(vmem_limit_bytes=VMEM_MOST),
        cost_estimate=SIX_US,
        name="kv_project",
    )(near, far, *pieces)


def kv_finish_kernel(one_ref, two_ref, bias_ref, cos_ref, sin_ref, o_ref):
    kv = one_ref[...] + two_ref[...] + bias_ref[:, :1]
    first, second = kv[:64], kv[64:]
    cos, sin = cos_ref[...], sin_ref[...]
    o_ref[0:64] = (first * cos - second * sin).astype(BF)
    o_ref[64:128] = (second * cos + first * sin).astype(BF)


def kv_finish(one, two, bias, cos, sin):
    inputs = [one, two, bias, cos, sin]
    return pl.pallas_call(
        kv_finish_kernel,
        in_specs=[full(v.shape) for v in inputs],
        out_specs=full(one.shape),
        out_shape=jax.ShapeDtypeStruct(one.shape, BF),
        compiler_params=pltpu.CompilerParams(vmem_limit_bytes=8 << 20),
        cost_estimate=CHEAP,
        name="kv_finish",
    )(*inputs)


def q_kernel(first, near_ref, far_ref, *refs):
    w_refs, refs = refs[:4], refs[4:]
    if first:
        so_far, refs = refs[:2], refs[2:]
    own_ref, other_ref, nbuf, wbuf, nsem, wsem = refs
    fetch((near_ref, far_ref), range(first, first + 4), nbuf, nsem, w_refs, wbuf, wsem)
    for t, o_ref in ((0, own_ref), (1, other_ref)):
        o_ref[...] = so_far[t][...] if first else jnp.zeros_like(o_ref)

    def step(i, carry):
        for r in range(2):
            pltpu.make_async_copy(w_refs[0], wbuf.at[2 * i + r], wsem.at[2 * i + r]).wait()
        for t, o_ref in ((0, own_ref), (1, other_ref)):
            out = None
            for r in range(2):
                k = 2 * i + r
                pltpu.make_async_copy(near_ref.at[0], nbuf.at[t, k], nsem.at[t, k]).wait()
                part = jnp.dot(nbuf[t, k], wbuf[k], preferred_element_type=F32)
                out = part if out is None else out + part
            o_ref[...] += out
        return carry

    lax.fori_loop(0, 2, step, 0)


def q_project(first, near, far, pieces, so_far):
    parts, rows, width = near.shape
    shape = jax.ShapeDtypeStruct((rows, 256), F32)
    return pl.pallas_call(
        functools.partial(q_kernel, first),
        in_specs=[HBM] * 6 + [full(shape.shape)] * len(so_far),
        out_specs=[full(shape.shape)] * 2,
        out_shape=[shape] * 2,
        scratch_shapes=[
            pltpu.VMEM((2, 4, rows, width), BF),
            pltpu.VMEM((4, 512, 256), BF),
            pltpu.SemaphoreType.DMA((2, 4)),
            pltpu.SemaphoreType.DMA((4,)),
        ],
        compiler_params=pltpu.CompilerParams(vmem_limit_bytes=VMEM_MOST),
        cost_estimate=THREE_US,
        name="q_project",
    )(near, far, *pieces, *so_far)


def choose_kernel(row_tab, col_tab, *refs):
    sources, outs = refs[:4], refs[4:]
    for f in range(4):
        for e in range(4):

            @pl.when(row_tab[f] == e)
            def _():
                outs[f][...] = sources[e][col_tab[f]]


def choose(row_tab, col_tab, sources):
    shape = sources[0].shape
    return pl.pallas_call(
        choose_kernel,
        grid_spec=pltpu.PrefetchScalarGridSpec(
            num_scalar_prefetch=2,
            grid=(1,),
            in_specs=[full(shape)] * 4,
            out_specs=[full(shape[1:])] * 4,
        ),
        out_shape=[jax.ShapeDtypeStruct(shape[1:], BF)] * 4,
        compiler_params=pltpu.CompilerParams(vmem_limit_bytes=8 << 20),
        cost_estimate=CHEAP,
        name="choose",
    )(row_tab, col_tab, *sources)


def q_finish_kernel(order, one_ref, two_ref, bias_ref, cos_ref, sin_ref, *outs):
    for d, o_ref in enumerate(outs):
        rows = pl.ds(pl.multiple_of(order[d] * 128, 128), 128)
        for h in range(2):
            cols = slice(h * 128, (h + 1) * 128)
            u = one_ref[rows, cols] + two_ref[rows, cols] + bias_ref[0:1, cols].astype(F32)
            o_ref[:, cols] = (u * cos_ref[rows, :] + pltpu.roll(u, 64, 1) * sin_ref[rows, :]).astype(BF)


def q_finish(order, one, two, bias, cos, sin):
    inputs = [one, two, bias, cos, sin]
    return pl.pallas_call(
        q_finish_kernel,
        grid_spec=pltpu.PrefetchScalarGridSpec(
            num_scalar_prefetch=1,
            grid=(1,),
            in_specs=[full(v.shape) for v in inputs],
            out_specs=[full((128, 256))] * 4,
        ),
        out_shape=[jax.ShapeDtypeStruct((128, 256), BF)] * 4,
        compiler_params=pltpu.CompilerParams(vmem_limit_bytes=8 << 20),
        cost_estimate=CHEAP,
        name="q_finish",
    )(order, *inputs)


def assemble_kernel(tab, *refs):
    o_ref = refs[4]
    for a in range(4):
        col = pl.multiple_of(tab[8 + a] * 512, 512)
        for i in range(2):
            o_ref[i, :, pl.ds(col, 512)] = refs[a][tab[5] ^ i]


def assemble(tab, base):
    shape = jax.ShapeDtypeStruct((2, 128, 2048), BF)
    return pl.pallas_call(
        assemble_kernel,
        grid_spec=pltpu.PrefetchScalarGridSpec(
            num_scalar_prefetch=1,
            grid=(1,),
            in_specs=[full(a.shape) for a in base],
            out_specs=full(shape.shape),
        ),
        out_shape=shape,
        compiler_params=pltpu.CompilerParams(vmem_limit_bytes=8 << 20),
        cost_estimate=CHEAP,
        name="assemble",
    )(tab, *base)


def attention_kernel(tab, q0, q1, q2, q3, own_ref, near_ref, far_ref, o_ref, qs, kv, sems):
    core, value_side = tab[4], tab[5]
    copies = [
        pltpu.make_async_copy(ref, kv.at[place_at], sems.at[i])
        for i, (ref, place_at) in enumerate(((near_ref, core), (far_ref, 1 - core)))
    ]
    for copy in copies:
        copy.start()
    own_kt = own_ref.at[value_side]
    own_vt = own_ref.at[value_side ^ 1]
    for f, q_ref in enumerate((q0, q1, q2, q3)):
        where = tab[12 + f]
        off = pl.multiple_of(lax.rem(where, 2) * 128, 128)
        for h in range(2):
            qs[where // 2, pl.ds(h * 256 + off, 128), :] = q_ref[:, h * 128 : (h + 1) * 128]

    factor = (128 ** -0.5) * math.log2(math.e)

    def lanes(p):
        total = p[:, :128]
        for i in range(1, p.shape[1] // 128):
            total = total + p[:, i * 128 : (i + 1) * 128]
        return total

    def pv(p, v):
        return lax.dot_general(p.astype(BF), v, (((1,), (1,)), ((), ())), preferred_element_type=F32)

    def first(blk):
        live = tab[2 + blk]
        c0 = blk * 256
        s = jnp.dot(qs[blk], own_kt[:, c0 : c0 + 256], preferred_element_type=F32) * factor
        row = lax.broadcasted_iota(jnp.int32, (512, 256), 0)
        row = jnp.where(row >= 256, row - 256, row)
        column = lax.broadcasted_iota(jnp.int32, (512, 256), 1)
        mask = (column <= row) & (column < live)
        s = jnp.where(mask, s, -1e30)
        top = jnp.max(s, axis=1, keepdims=True)
        p = jnp.where(mask, jnp.exp2(s - top), 0.0)
        return (top, lanes(p), pv(p, own_vt[:, c0 : c0 + 256]))

    def wide(blk, i, state):
        top, total, acc = state
        keys = pl.ds(pl.multiple_of(i * 512, 512), 512)
        ss = [jnp.dot(qs[blk], kv[side, 0, :, keys], preferred_element_type=F32) * factor for side in range(2)]
        new = jnp.maximum(top, jnp.max(jnp.maximum(ss[0], ss[1]), axis=1, keepdims=True))
        ps = [jnp.exp2(s - new) for s in ss]
        decay = jnp.exp2(top - new)
        total = total * decay + (lanes(ps[0]) + lanes(ps[1]))
        return (new, total, acc * decay + (pv(ps[0], kv[0, 1, :, keys]) + pv(ps[1], kv[1, 1, :, keys])))

    def step(blk, c, width, state):
        top, total, acc = state
        side = lax.rem(c, 2)
        keys = pl.ds(pl.multiple_of(c // 2 * 512, 512), width)
        s = jnp.dot(qs[blk], kv[side, 0, :, keys], preferred_element_type=F32) * factor
        new = jnp.maximum(top, jnp.max(s, axis=1, keepdims=True))
        p = jnp.exp2(s - new)
        decay = jnp.exp2(top - new)
        return (new, total * decay + lanes(p), acc * decay + pv(p, kv[side, 1, :, keys]))

    states = [first(0), first(1)]
    for copy in copies:
        copy.wait()
    for blk in range(2):
        n = tab[blk]
        state = lax.fori_loop(0, n // 4, lambda i, st: wide(blk, i, st), states[blk])
        state = lax.fori_loop(n // 4 * 2, n // 2, lambda c, st: step(blk, c, 512, st), state)
        state = lax.fori_loop(0, lax.rem(n, 2), lambda i, st: step(blk, n // 2, 256, st), state)
        top, total, acc = state
        result = (acc / jnp.sum(total, axis=1, keepdims=True)).astype(BF)
        for h in range(2):
            o_ref[blk * 256 : (blk + 1) * 256, h * 128 : (h + 1) * 128] = result[h * 256 : (h + 1) * 256]


def attention(tab, candidates, own, near, far):
    inputs = [*candidates, own]
    return pl.pallas_call(
        attention_kernel,
        grid_spec=pltpu.PrefetchScalarGridSpec(
            num_scalar_prefetch=1,
            grid=(1,),
            in_specs=[full(a.shape) for a in inputs] + [HBM] * 2,
            out_specs=full((512, 256)),
            scratch_shapes=[
                pltpu.VMEM((2, 512, 128), BF),
                pltpu.VMEM((2, 2, 128, 2048), BF),
                pltpu.SemaphoreType.DMA((2,)),
            ],
        ),
        out_shape=jax.ShapeDtypeStruct((512, 256), BF),
        compiler_params=pltpu.CompilerParams(vmem_limit_bytes=VMEM_LIMIT),
        cost_estimate=CHEAP,
        name="attention",
    )(tab, *inputs, near, far)


def shift(v, axis, by):
    n = lax.axis_size(axis)
    return lax.ppermute(v, axis, [(i, (i + by) % n) for i in range(n)])


def flip(v, axis, bits):
    n = lax.axis_size(axis)
    return lax.ppermute(v, axis, [(i, i ^ bits) for i in range(n)])


def after(value, *others):
    return lax.optimization_barrier((value, *others))[0]


def each(fn, values, *others):
    return [fn(after(v, *others) if others else v) for v in values]


def local(
    hidden,
    norm_gain,
    trainer_query,
    trainer_query_bias,
    trainer_kv,
    trainer_kv_bias,
    matching,
    block_lists,
    completion_lengths,
):
    zh, x, core, y, zl = (lax.axis_index(a).astype(jnp.int32) for a in (ZH, X, CORE, Y, ZL))
    rows = hidden.shape[0]
    ctx = (zh * 4 + x) * 2 + core
    four = jnp.arange(4, dtype=jnp.int32)

    ks = jnp.arange(16, dtype=jnp.int32)
    order = ((zh ^ ((ks >> 2) & 1)) * 4 + (x ^ (ks & 3))) * 2 + (core ^ (ks >> 3))
    near, far_out = norm(hidden, norm_gain, order)

    value_side = zl & 1
    half_at = lambda v: lax.dynamic_slice_in_dim(
        lax.dynamic_index_in_dim(v, y, 0, keepdims=False), value_side * 128, 128, v.ndim - 2
    )
    packed = half_at(trainer_kv)
    own_bias = jnp.broadcast_to(half_at(trainer_kv_bias).astype(F32)[:, None], (128, 128))

    s0 = trainer_query[0]
    z0 = flip(s0, ZH, 1)
    both = jnp.stack([packed, flip(packed, ZH, 1)])
    s_near = [s0] + [flip(s0, X, d) for d in (1, 2, 3)]
    near, far_out, z0, both, *s_near = lax.optimization_barrier((near, far_out, z0, both, *s_near))
    far = flip(far_out, CORE, 1)
    p_near = [both] + [flip(both, X, d) for d in (1, 2, 3)]
    z0 = after(z0, p_near[1])
    z_near = [z0] + [flip(z0, X, d) for d in (1, 2, 3)]

    counts = jnp.sum((block_lists >= 0).astype(jnp.int32), axis=1)
    token = jnp.arange(rows, dtype=jnp.int32)
    positions = (jnp.where(token < BLK, counts[0], counts[1]) - 1) * BLK + token % BLK
    freqs = THETA ** (-2.0 * jnp.arange(64, dtype=F32) / 128)
    angles = positions.astype(F32)[:, None] * freqs[None, :]
    cosine, sine = jnp.cos(angles), jnp.sin(angles)
    cos2 = jnp.concatenate([cosine, cosine], axis=1)
    sin2 = jnp.concatenate([-sine, sine], axis=1)
    cos_t = jnp.where(value_side == 0, cosine.T, 1.0)
    sin_t = jnp.where(value_side == 0, sine.T, 0.0)

    q_half = list(q_project(0, near, far, s_near, []))
    kv_own, kv_other = kv_project(after(near, q_half[0]), far, p_near)
    kv_other, q_half[0], *z_near = lax.optimization_barrier((kv_other, q_half[0], *z_near))
    piece = kv_finish(kv_own, flip(kv_other, CORE, 1), own_bias, cos_t, sin_t)
    over = flip(piece, ZH, 1)
    start = jnp.where(zh == 0, piece, over)
    pair = jnp.stack([start, piece])
    mate = flip(pair, ZL, 1)
    base0 = jnp.stack([pair[0], mate[0]])
    own = jnp.stack([pair[1], mate[1]])

    q_own, q_other = q_project(4, near, far, z_near, q_half)
    parts = q_finish(zl ^ four, q_own, flip(q_other, CORE, 1), trainer_query_bias, cos2, sin2)
    mine = jnp.stack([parts[0]] + [flip(parts[d], ZL, d) for d in (1, 2, 3)])
    mine, base0 = lax.optimization_barrier((mine, base0))
    gathered = [mine] + [flip(mine, Y, e) for e in (1, 2, 3)]
    base_near = [base0] + [flip(base0, X, d) for d in (1, 2, 3)]
    target = y * 4 + (zl ^ four)
    src = jnp.sum(
        jnp.where(matching[None, :] == target[:, None], jnp.arange(16, dtype=jnp.int32)[None, :], 0), axis=1
    )
    tab_1 = ((src // 4) ^ y).astype(jnp.int32)
    tab_1, *base_near = lax.optimization_barrier((tab_1, *base_near))
    sent = choose(tab_1, ((src % 4) ^ zl).astype(jnp.int32), gathered)
    base_near[0] = after(base_near[0], sent[0])
    candidates = [sent[0]] + [flip(sent[f], ZL, f) for f in (1, 2, 3)]

    blocks = ctx * 2 + jnp.arange(2, dtype=jnp.int32)
    slots = jnp.arange(16, dtype=jnp.int32)
    lengths = jnp.sum(
        jnp.where((blocks[:, None] - 16) == slots[None, :], completion_lengths[None, :], 0), axis=1
    )
    live = jnp.where(blocks < 16, BLK, lengths)
    tab = jnp.concatenate(
        [
            counts - 1,
            live,
            core[None],
            value_side[None],
            jnp.zeros((2,), jnp.int32),
            x ^ four,
            zl ^ four,
        ]
    ).astype(jnp.int32)
    whole = assemble(tab, base_near)
    return attention(tab, candidates, own, whole, flip(whole, CORE, 1))


def solution(mesh):
    fine = Mesh(mesh.devices.reshape(2, 4, 2, 4, 4), (ZH, X, CORE, Y, ZL))
    ctx = (ZH, X, CORE)
    tp = (Y, ZL)
    in_specs = (
        P(ctx, None),
        P(),
        P(tp, ctx, None),
        P(tp, None),
        P(None, ctx, None),
        P(),
        P(),
        P(ctx, None),
        P(),
    )
    return jax.shard_map(local, mesh=fine, in_specs=in_specs, out_specs=P(ctx, tp), check_vma=False)
```

```python
import functools
import math

import jax
import jax.numpy as jnp
from jax import lax
from jax.experimental import pallas as pl
from jax.experimental.pallas import tpu as pltpu
from jax.sharding import Mesh, PartitionSpec as P

BLK = 256
THETA = 1000000.0
EPSILON = 1e-06
BF = jnp.bfloat16
F32 = jnp.float32
ZH, X, CORE, Y, ZL = "zh", "x", "core", "y", "zl"


def full(shape):
    zeros = (0,) * len(shape)
    return pl.BlockSpec(shape, lambda *_: zeros)


CHEAP = pl.CostEstimate(flops=0, bytes_accessed=0, transcendentals=0)
SIX_US = pl.CostEstimate(flops=0, bytes_accessed=20 << 20, transcendentals=0)
HBM = pl.BlockSpec(memory_space=pltpu.HBM)
VMEM_LIMIT = 40 << 20
VMEM_MOST = 60 << 20


THREE_US = pl.CostEstimate(flops=0, bytes_accessed=10 << 20, transcendentals=0)


def norm_kernel(order, h_hbm, g_ref, near_hbm, far_hbm, hbuf, near, far, in_sem, out_sem):
    parts, rows, width = near.shape
    count, step, _ = hbuf.shape

    def load(i):
        return pltpu.make_async_copy(h_hbm.at[pl.ds(i * step, step)], hbuf.at[i], in_sem.at[i])

    def store(i, t):
        here, there = ((near, near_hbm), (far, far_hbm))[t]
        rows_i = pl.ds(pl.multiple_of(i * step, step), step)
        return pltpu.make_async_copy(here.at[:, rows_i], there.at[:, rows_i], out_sem.at[t, i])

    for i in range(count):
        load(i).start()

    def block(i, carry):
        pltpu.make_async_copy(h_hbm.at[pl.ds(0, step)], hbuf.at[i], in_sem.at[i]).wait()

        def square(k, total):
            piece = hbuf[i, :, pl.ds(pl.multiple_of(k * width, width), width)].astype(F32)
            return total + piece * piece

        total = lax.fori_loop(0, 2 * parts, square, jnp.zeros((step, width), F32), unroll=4)
        mean = jnp.sum(total, axis=1, keepdims=True) * (1.0 / (2 * parts * width))
        rs = lax.rsqrt(mean + EPSILON)
        rows_i = pl.ds(pl.multiple_of(i * step, step), step)
        for t, half, o_ref in ((0, 0, near), (1, parts, far)):

            def scale(k, inner):
                off = pl.multiple_of(order[half + k] * width, width)
                piece = hbuf[i, :, pl.ds(off, width)].astype(F32)
                gain = g_ref[:, pl.ds(off, width)].astype(F32)
                o_ref[k, rows_i, :] = (piece * rs * gain).astype(BF)
                return inner

            lax.fori_loop(0, parts, scale, 0, unroll=4)
            store(i, t).start()
        return carry

    lax.fori_loop(0, count, block, 0)
    for i in range(count):
        for t in range(2):
            store(i, t).wait()


def norm(hidden, gain, order):
    rows, d = hidden.shape
    parts = 8
    width = d // parts // 2
    step = 64
    count = rows // step
    shape = jax.ShapeDtypeStruct((parts, rows, width), BF)
    return pl.pallas_call(
        norm_kernel,
        grid_spec=pltpu.PrefetchScalarGridSpec(
            num_scalar_prefetch=1,
            grid=(1,),
            in_specs=[HBM, full((1, d))],
            out_specs=[HBM, HBM],
            scratch_shapes=[
                pltpu.VMEM((count, step, d), BF),
                pltpu.VMEM(shape.shape, BF),
                pltpu.VMEM(shape.shape, BF),
                pltpu.SemaphoreType.DMA((count,)),
                pltpu.SemaphoreType.DMA((2, count)),
            ],
        ),
        out_shape=[shape] * 2,
        compiler_params=pltpu.CompilerParams(vmem_limit_bytes=VMEM_MOST),
        cost_estimate=SIX_US,
        name="norm",
    )(order, hidden, gain.reshape(1, d))


def tokens(n_refs, k, nbuf, nsem, j):
    rows = nbuf.shape[1] // 2
    return [
        pltpu.make_async_copy(n_ref.at[k], nbuf.at[j, pl.ds(t * rows, rows)], nsem.at[t, j])
        for t, n_ref in enumerate(n_refs)
    ]


def kv_kernel(near_ref, far_ref, *refs):
    w_refs = refs[:4]
    own_ref, other_ref, nbuf, wbuf, acc, nsem, wsem = refs[4:]
    load = lambda i, r: tokens((near_ref, far_ref), i + 4 * r, nbuf, nsem, 2 * i + r)
    for i, w_ref in enumerate(w_refs):
        pltpu.make_async_copy(w_ref, wbuf.at[i], wsem.at[i]).start()
        if i == 0:
            for r in range(2):
                for copy in load(0, r):
                    copy.start()
    acc[...] = jnp.zeros_like(acc)

    def step(i, carry):
        @pl.when(i < 3)
        def _():
            for r in range(2):
                for copy in load(i + 1, r):
                    copy.start()

        pltpu.make_async_copy(w_refs[0], wbuf.at[i], wsem.at[i]).wait()
        out = None
        for r in range(2):
            for copy in load(i, r):
                copy.wait()
            part = jnp.dot(nbuf[2 * i + r], wbuf[i, r], preferred_element_type=F32)
            out = part if out is None else out + part
        acc[...] += out
        return carry

    lax.fori_loop(0, 4, step, 0)
    own_ref[...] = acc[:512].T
    other_ref[...] = acc[512:].T


def kv_project(near, far, pieces):
    parts, rows, width = near.shape
    return pl.pallas_call(
        kv_kernel,
        in_specs=[HBM] * 6,
        out_specs=[full((128, rows))] * 2,
        out_shape=[jax.ShapeDtypeStruct((128, rows), F32)] * 2,
        scratch_shapes=[
            pltpu.VMEM((parts, 2 * rows, width), BF),
            pltpu.VMEM((4, 2, 512, 128), BF),
            pltpu.VMEM((2 * rows, 128), F32),
            pltpu.SemaphoreType.DMA((2, 8)),
            pltpu.SemaphoreType.DMA((4,)),
        ],
        compiler_params=pltpu.CompilerParams(vmem_limit_bytes=VMEM_MOST),
        cost_estimate=SIX_US,
        name="kv_project",
    )(near, far, *pieces)


def kv_finish_kernel(one_ref, two_ref, bias_ref, cos_ref, sin_ref, o_ref):
    kv = one_ref[...] + two_ref[...] + bias_ref[:, :1]
    first, second = kv[:64], kv[64:]
    cos, sin = cos_ref[...], sin_ref[...]
    o_ref[0:64] = (first * cos - second * sin).astype(BF)
    o_ref[64:128] = (second * cos + first * sin).astype(BF)


def kv_finish(one, two, bias, cos, sin):
    inputs = [one, two, bias, cos, sin]
    return pl.pallas_call(
        kv_finish_kernel,
        in_specs=[full(v.shape) for v in inputs],
        out_specs=full(one.shape),
        out_shape=jax.ShapeDtypeStruct(one.shape, BF),
        compiler_params=pltpu.CompilerParams(vmem_limit_bytes=8 << 20),
        cost_estimate=CHEAP,
        name="kv_finish",
    )(*inputs)


def q_kernel(first, near_ref, far_ref, *refs):
    w_refs, refs = refs[:4], refs[4:]
    so_far, refs = refs[:-9], refs[-9:]
    own_ref, other_ref, nbuf, wbuf, acc, nsem, wsem, before, bsem = refs
    rows = own_ref.shape[0]
    load = lambda k: tokens((near_ref, far_ref), first + k, nbuf, nsem, k)
    for k, w_ref in enumerate(w_refs):
        pltpu.make_async_copy(w_ref, wbuf.at[k], wsem.at[k]).start()
        if k < 2:
            for copy in load(k):
                copy.start()

    earlier = [pltpu.make_async_copy(ref, before.at[t], bsem.at[t]) for t, ref in enumerate(so_far)]
    for copy in earlier:
        copy.start()

    def part(i):
        out = None
        for r in range(2):
            k = 2 * i + r
            if k < 2:
                for copy in load(k + 2):
                    copy.start()
            pltpu.make_async_copy(w_refs[0], wbuf.at[k], wsem.at[k]).wait()
            for copy in load(k):
                copy.wait()
            one = jnp.dot(nbuf[k], wbuf[k], preferred_element_type=F32)
            out = one if out is None else out + one
        return out

    acc[...] = part(0)
    total = acc[...] + part(1)
    for copy in earlier:
        copy.wait()
    for t, o_ref in ((0, own_ref), (1, other_ref)):
        half = total[t * rows : (t + 1) * rows]
        o_ref[...] = half + before[t] if so_far else half


def q_project(first, near, far, pieces, so_far):
    parts, rows, width = near.shape
    shape = jax.ShapeDtypeStruct((rows, 256), F32)
    return pl.pallas_call(
        functools.partial(q_kernel, first),
        in_specs=[HBM] * (6 + len(so_far)),
        out_specs=[full(shape.shape)] * 2,
        out_shape=[shape] * 2,
        scratch_shapes=[
            pltpu.VMEM((4, 2 * rows, width), BF),
            pltpu.VMEM((4, 512, 256), BF),
            pltpu.VMEM((2 * rows, 256), F32),
            pltpu.SemaphoreType.DMA((2, 4)),
            pltpu.SemaphoreType.DMA((4,)),
            pltpu.VMEM((2, rows, 256), F32),
            pltpu.SemaphoreType.DMA((2,)),
        ],
        compiler_params=pltpu.CompilerParams(vmem_limit_bytes=VMEM_MOST),
        cost_estimate=THREE_US,
        name="q_project",
    )(near, far, *pieces, *so_far)


def choose_kernel(row_tab, col_tab, *refs):
    sources, outs = refs[:4], refs[4:]
    for f in range(4):
        for e in range(4):

            @pl.when(row_tab[f] == e)
            def _():
                outs[f][...] = sources[e][col_tab[f]]


def choose(row_tab, col_tab, sources):
    shape = sources[0].shape
    return pl.pallas_call(
        choose_kernel,
        grid_spec=pltpu.PrefetchScalarGridSpec(
            num_scalar_prefetch=2,
            grid=(1,),
            in_specs=[full(shape)] * 4,
            out_specs=[full(shape[1:])] * 4,
        ),
        out_shape=[jax.ShapeDtypeStruct(shape[1:], BF)] * 4,
        compiler_params=pltpu.CompilerParams(vmem_limit_bytes=8 << 20),
        cost_estimate=CHEAP,
        name="choose",
    )(row_tab, col_tab, *sources)


def q_finish_kernel(order, one_ref, two_ref, bias_ref, cos_ref, sin_ref, *outs):
    for d, o_ref in enumerate(outs):
        rows = pl.ds(pl.multiple_of(order[d] * 128, 128), 128)
        for h in range(2):
            cols = slice(h * 128, (h + 1) * 128)
            u = one_ref[rows, cols] + two_ref[rows, cols] + bias_ref[0:1, cols].astype(F32)
            o_ref[:, cols] = (u * cos_ref[rows, :] + pltpu.roll(u, 64, 1) * sin_ref[rows, :]).astype(BF)


def q_finish(order, one, two, bias, cos, sin):
    inputs = [one, two, bias, cos, sin]
    return pl.pallas_call(
        q_finish_kernel,
        grid_spec=pltpu.PrefetchScalarGridSpec(
            num_scalar_prefetch=1,
            grid=(1,),
            in_specs=[full(v.shape) for v in inputs],
            out_specs=[full((128, 256))] * 4,
        ),
        out_shape=[jax.ShapeDtypeStruct((128, 256), BF)] * 4,
        compiler_params=pltpu.CompilerParams(vmem_limit_bytes=8 << 20),
        cost_estimate=CHEAP,
        name="q_finish",
    )(order, *inputs)


def assemble_kernel(tab, *refs):
    o_ref = refs[4]
    for a in range(4):
        col = pl.multiple_of(tab[8 + a] * 512, 512)
        for i in range(2):
            o_ref[i, :, pl.ds(col, 512)] = refs[a][tab[5] ^ i]


def assemble(tab, base):
    shape = jax.ShapeDtypeStruct((2, 128, 2048), BF)
    return pl.pallas_call(
        assemble_kernel,
        grid_spec=pltpu.PrefetchScalarGridSpec(
            num_scalar_prefetch=1,
            grid=(1,),
            in_specs=[full(a.shape) for a in base],
            out_specs=full(shape.shape),
        ),
        out_shape=shape,
        compiler_params=pltpu.CompilerParams(vmem_limit_bytes=8 << 20),
        cost_estimate=CHEAP,
        name="assemble",
    )(tab, *base)


def attention_kernel(tab, q0, q1, q2, q3, own_ref, near_ref, far_ref, o_ref, qs, kv, sems):
    core, value_side = tab[4], tab[5]
    copies = [
        pltpu.make_async_copy(ref, kv.at[place_at], sems.at[i])
        for i, (ref, place_at) in enumerate(((near_ref, core), (far_ref, 1 - core)))
    ]
    for copy in copies:
        copy.start()
    own_kt = own_ref.at[value_side]
    own_vt = own_ref.at[value_side ^ 1]
    for f, q_ref in enumerate((q0, q1, q2, q3)):
        where = tab[12 + f]
        off = pl.multiple_of(lax.rem(where, 2) * 128, 128)
        for h in range(2):
            qs[where // 2, pl.ds(h * 256 + off, 128), :] = q_ref[:, h * 128 : (h + 1) * 128]

    factor = (128 ** -0.5) * math.log2(math.e)

    def lanes(p):
        total = p[:, :128]
        for i in range(1, p.shape[1] // 128):
            total = total + p[:, i * 128 : (i + 1) * 128]
        return total

    def pv(p, v):
        return lax.dot_general(p.astype(BF), v, (((1,), (1,)), ((), ())), preferred_element_type=F32)

    def first(blk):
        live = tab[2 + blk]
        c0 = blk * 256
        s = jnp.dot(qs[blk], own_kt[:, c0 : c0 + 256], preferred_element_type=F32) * factor
        row = lax.broadcasted_iota(jnp.int32, (512, 256), 0)
        row = jnp.where(row >= 256, row - 256, row)
        column = lax.broadcasted_iota(jnp.int32, (512, 256), 1)
        mask = (column <= row) & (column < live)
        s = jnp.where(mask, s, -1e30)
        top = jnp.max(s, axis=1, keepdims=True)
        p = jnp.where(mask, jnp.exp2(s - top), 0.0)
        return (top, lanes(p), pv(p, own_vt[:, c0 : c0 + 256]))

    def wide(blk, i, state):
        top, total, acc = state
        keys = pl.ds(pl.multiple_of(i * 512, 512), 512)
        ss = [jnp.dot(qs[blk], kv[side, 0, :, keys], preferred_element_type=F32) * factor for side in range(2)]
        new = jnp.maximum(top, jnp.max(jnp.maximum(ss[0], ss[1]), axis=1, keepdims=True))
        ps = [jnp.exp2(s - new) for s in ss]
        decay = jnp.exp2(top - new)
        total = total * decay + (lanes(ps[0]) + lanes(ps[1]))
        return (new, total, acc * decay + (pv(ps[0], kv[0, 1, :, keys]) + pv(ps[1], kv[1, 1, :, keys])))

    def step(blk, c, width, state):
        top, total, acc = state
        side = lax.rem(c, 2)
        keys = pl.ds(pl.multiple_of(c // 2 * 512, 512), width)
        s = jnp.dot(qs[blk], kv[side, 0, :, keys], preferred_element_type=F32) * factor
        new = jnp.maximum(top, jnp.max(s, axis=1, keepdims=True))
        p = jnp.exp2(s - new)
        decay = jnp.exp2(top - new)
        return (new, total * decay + lanes(p), acc * decay + pv(p, kv[side, 1, :, keys]))

    states = [first(0), first(1)]
    for copy in copies:
        copy.wait()
    for blk in range(2):
        n = tab[blk]
        state = lax.fori_loop(0, n // 4, lambda i, st: wide(blk, i, st), states[blk])
        state = lax.fori_loop(n // 4 * 2, n // 2, lambda c, st: step(blk, c, 512, st), state)
        state = lax.fori_loop(0, lax.rem(n, 2), lambda i, st: step(blk, n // 2, 256, st), state)
        top, total, acc = state
        result = (acc / jnp.sum(total, axis=1, keepdims=True)).astype(BF)
        for h in range(2):
            o_ref[blk * 256 : (blk + 1) * 256, h * 128 : (h + 1) * 128] = result[h * 256 : (h + 1) * 256]


def attention(tab, candidates, own, near, far):
    inputs = [*candidates, own]
    return pl.pallas_call(
        attention_kernel,
        grid_spec=pltpu.PrefetchScalarGridSpec(
            num_scalar_prefetch=1,
            grid=(1,),
            in_specs=[full(a.shape) for a in inputs] + [HBM] * 2,
            out_specs=full((512, 256)),
            scratch_shapes=[
                pltpu.VMEM((2, 512, 128), BF),
                pltpu.VMEM((2, 2, 128, 2048), BF),
                pltpu.SemaphoreType.DMA((2,)),
            ],
        ),
        out_shape=jax.ShapeDtypeStruct((512, 256), BF),
        compiler_params=pltpu.CompilerParams(vmem_limit_bytes=VMEM_LIMIT),
        cost_estimate=CHEAP,
        name="attention",
    )(tab, *inputs, near, far)


def shift(v, axis, by):
    n = lax.axis_size(axis)
    return lax.ppermute(v, axis, [(i, (i + by) % n) for i in range(n)])


def flip(v, axis, bits):
    n = lax.axis_size(axis)
    return lax.ppermute(v, axis, [(i, i ^ bits) for i in range(n)])


def after(value, *others):
    return lax.optimization_barrier((value, *others))[0]


def each(fn, values, *others):
    return [fn(after(v, *others) if others else v) for v in values]


def local(
    hidden,
    norm_gain,
    trainer_query,
    trainer_query_bias,
    trainer_kv,
    trainer_kv_bias,
    matching,
    block_lists,
    completion_lengths,
):
    zh, x, core, y, zl = (lax.axis_index(a).astype(jnp.int32) for a in (ZH, X, CORE, Y, ZL))
    rows = hidden.shape[0]
    ctx = (zh * 4 + x) * 2 + core
    four = jnp.arange(4, dtype=jnp.int32)

    ks = jnp.arange(16, dtype=jnp.int32)
    order = ((zh ^ ((ks >> 2) & 1)) * 4 + (x ^ (ks & 3))) * 2 + (core ^ (ks >> 3))
    near, far_out = norm(hidden, norm_gain, order)

    value_side = zl & 1
    half_at = lambda v: lax.dynamic_slice_in_dim(
        lax.dynamic_index_in_dim(v, y, 0, keepdims=False), value_side * 128, 128, v.ndim - 2
    )
    packed = half_at(trainer_kv)
    own_bias = jnp.broadcast_to(half_at(trainer_kv_bias).astype(F32)[:, None], (128, 128))

    s0 = trainer_query[0]
    z0 = flip(s0, ZH, 1)
    both = jnp.stack([packed, flip(packed, ZH, 1)])
    s_near = [s0] + [flip(s0, X, d) for d in (1, 2, 3)]
    near, far_out, z0, both, *s_near = lax.optimization_barrier((near, far_out, z0, both, *s_near))
    far = flip(far_out, CORE, 1)
    p_near = [both] + [flip(both, X, d) for d in (1, 2, 3)]
    z0 = after(z0, p_near[1])
    z_near = [z0] + [flip(z0, X, d) for d in (1, 2, 3)]

    q_half = list(q_project(0, near, far, s_near, []))
    kv_own, kv_other = kv_project(after(near, q_half[0]), far, p_near)
    counts = jnp.sum((after(block_lists, kv_own) >= 0).astype(jnp.int32), axis=1)
    token = jnp.arange(rows, dtype=jnp.int32)
    positions = (jnp.where(token < BLK, counts[0], counts[1]) - 1) * BLK + token % BLK
    freqs = THETA ** (-2.0 * jnp.arange(64, dtype=F32) / 128)
    angles = positions.astype(F32)[:, None] * freqs[None, :]
    cosine, sine = jnp.cos(angles), jnp.sin(angles)
    cos2 = jnp.concatenate([cosine, cosine], axis=1)
    sin2 = jnp.concatenate([-sine, sine], axis=1)
    cos_t = jnp.where(value_side == 0, cosine.T, 1.0)
    sin_t = jnp.where(value_side == 0, sine.T, 0.0)

    kv_other, q_half[0], cos_t, sin_t, cos2, sin2, *z_near = lax.optimization_barrier(
        (kv_other, q_half[0], cos_t, sin_t, cos2, sin2, *z_near)
    )
    piece = kv_finish(kv_own, flip(kv_other, CORE, 1), own_bias, cos_t, sin_t)
    over = flip(piece, ZH, 1)
    start = jnp.where(zh == 0, piece, over)
    pair = jnp.stack([start, piece])
    mate = flip(pair, ZL, 1)
    base0 = jnp.stack([pair[0], mate[0]])
    own = jnp.stack([pair[1], mate[1]])

    q_own, q_other = q_project(4, near, far, z_near, q_half)
    parts = q_finish(zl ^ four, q_own, flip(q_other, CORE, 1), trainer_query_bias, cos2, sin2)
    mine = jnp.stack([parts[0]] + [flip(parts[d], ZL, d) for d in (1, 2, 3)])
    mine, base0 = lax.optimization_barrier((mine, base0))
    gathered = [mine] + [flip(mine, Y, e) for e in (1, 2, 3)]
    base_near = [base0] + [flip(base0, X, d) for d in (1, 2, 3)]
    target = y * 4 + (zl ^ four)
    src = jnp.sum(
        jnp.where(matching[None, :] == target[:, None], jnp.arange(16, dtype=jnp.int32)[None, :], 0), axis=1
    )
    tab_1 = ((src // 4) ^ y).astype(jnp.int32)
    tab_1, *base_near = lax.optimization_barrier((tab_1, *base_near))
    sent = choose(tab_1, ((src % 4) ^ zl).astype(jnp.int32), gathered)
    base_near[0] = after(base_near[0], sent[0])
    candidates = [sent[0]] + [flip(sent[f], ZL, f) for f in (1, 2, 3)]

    blocks = ctx * 2 + jnp.arange(2, dtype=jnp.int32)
    slots = jnp.arange(16, dtype=jnp.int32)
    lengths = jnp.sum(
        jnp.where((blocks[:, None] - 16) == slots[None, :], completion_lengths[None, :], 0), axis=1
    )
    live = jnp.where(blocks < 16, BLK, lengths)
    tab = jnp.concatenate(
        [
            counts - 1,
            live,
            core[None],
            value_side[None],
            jnp.zeros((2,), jnp.int32),
            x ^ four,
            zl ^ four,
        ]
    ).astype(jnp.int32)
    whole = assemble(tab, base_near)
    return attention(tab, candidates, own, whole, flip(whole, CORE, 1))


def solution(mesh):
    fine = Mesh(mesh.devices.reshape(2, 4, 2, 4, 4), (ZH, X, CORE, Y, ZL))
    ctx = (ZH, X, CORE)
    tp = (Y, ZL)
    in_specs = (
        P(ctx, None),
        P(),
        P(tp, ctx, None),
        P(tp, None),
        P(None, ctx, None),
        P(),
        P(),
        P(ctx, None),
        P(),
    )
    return jax.shard_map(local, mesh=fine, in_specs=in_specs, out_specs=P(ctx, tp), check_vma=False)
```

```python
import functools
import math

import jax
import jax.numpy as jnp
from jax import lax
from jax.experimental import pallas as pl
from jax.experimental.pallas import tpu as pltpu
from jax.sharding import Mesh, PartitionSpec as P

BLK = 256
THETA = 1000000.0
EPSILON = 1e-06
BF = jnp.bfloat16
F32 = jnp.float32
ZH, X, CORE, Y, ZL = "zh", "x", "core", "y", "zl"


def full(shape):
    zeros = (0,) * len(shape)
    return pl.BlockSpec(shape, lambda *_: zeros)


CHEAP = pl.CostEstimate(flops=0, bytes_accessed=0, transcendentals=0)
SIX_US = pl.CostEstimate(flops=0, bytes_accessed=20 << 20, transcendentals=0)
HBM = pl.BlockSpec(memory_space=pltpu.HBM)
VMEM_LIMIT = 40 << 20
VMEM_MOST = 60 << 20


THREE_US = pl.CostEstimate(flops=0, bytes_accessed=10 << 20, transcendentals=0)


def norm_kernel(order, h_hbm, g_ref, near_hbm, far_hbm, hbuf, near, far, in_sem, out_sem):
    parts, rows, width = near.shape
    count, step, _ = hbuf.shape

    def load(i):
        return pltpu.make_async_copy(h_hbm.at[pl.ds(i * step, step)], hbuf.at[i], in_sem.at[i])

    def store(i, t):
        here, there = ((near, near_hbm), (far, far_hbm))[t]
        rows_i = pl.ds(pl.multiple_of(i * step, step), step)
        return pltpu.make_async_copy(here.at[:, rows_i], there.at[:, rows_i], out_sem.at[t, i])

    for i in range(count):
        load(i).start()

    def block(i, carry):
        pltpu.make_async_copy(h_hbm.at[pl.ds(0, step)], hbuf.at[i], in_sem.at[i]).wait()

        def square(k, total):
            piece = hbuf[i, :, pl.ds(pl.multiple_of(k * width, width), width)].astype(F32)
            return total + piece * piece

        total = lax.fori_loop(0, 2 * parts, square, jnp.zeros((step, width), F32), unroll=8)
        mean = jnp.sum(total, axis=1, keepdims=True) * (1.0 / (2 * parts * width))
        rs = lax.rsqrt(mean + EPSILON)
        rows_i = pl.ds(pl.multiple_of(i * step, step), step)
        for t, half, o_ref in ((0, 0, near), (1, parts, far)):

            def scale(k, inner):
                off = pl.multiple_of(order[half + k] * width, width)
                piece = hbuf[i, :, pl.ds(off, width)].astype(F32)
                gain = g_ref[:, pl.ds(off, width)].astype(F32)
                o_ref[k, rows_i, :] = (piece * rs * gain).astype(BF)
                return inner

            lax.fori_loop(0, parts, scale, 0, unroll=8)
            store(i, t).start()
        return carry

    lax.fori_loop(0, count, block, 0)
    for i in range(count):
        for t in range(2):
            store(i, t).wait()


def norm(hidden, gain, order):
    rows, d = hidden.shape
    parts = 8
    width = d // parts // 2
    step = 64
    count = rows // step
    shape = jax.ShapeDtypeStruct((parts, rows, width), BF)
    return pl.pallas_call(
        norm_kernel,
        grid_spec=pltpu.PrefetchScalarGridSpec(
            num_scalar_prefetch=1,
            grid=(1,),
            in_specs=[HBM, full((1, d))],
            out_specs=[HBM, HBM],
            scratch_shapes=[
                pltpu.VMEM((count, step, d), BF),
                pltpu.VMEM(shape.shape, BF),
                pltpu.VMEM(shape.shape, BF),
                pltpu.SemaphoreType.DMA((count,)),
                pltpu.SemaphoreType.DMA((2, count)),
            ],
        ),
        out_shape=[shape] * 2,
        compiler_params=pltpu.CompilerParams(vmem_limit_bytes=VMEM_MOST),
        cost_estimate=SIX_US,
        name="norm",
    )(order, hidden, gain.reshape(1, d))


def tokens(n_refs, k, nbuf, nsem, j):
    rows = nbuf.shape[1] // 2
    return [
        pltpu.make_async_copy(n_ref.at[k], nbuf.at[j, pl.ds(t * rows, rows)], nsem.at[t, j])
        for t, n_ref in enumerate(n_refs)
    ]


def kv_kernel(near_ref, far_ref, *refs):
    w_refs = refs[:4]
    own_ref, other_ref, nbuf, wbuf, acc, nsem, wsem = refs[4:]
    load = lambda i, r: tokens((near_ref, far_ref), i + 4 * r, nbuf, nsem, 2 * i + r)
    for i, w_ref in enumerate(w_refs):
        pltpu.make_async_copy(w_ref, wbuf.at[i], wsem.at[i]).start()
        if i == 0:
            for r in range(2):
                for copy in load(0, r):
                    copy.start()
    acc[...] = jnp.zeros_like(acc)

    def step(i, carry):
        @pl.when(i < 3)
        def _():
            for r in range(2):
                for copy in load(i + 1, r):
                    copy.start()

        pltpu.make_async_copy(w_refs[0], wbuf.at[i], wsem.at[i]).wait()
        out = None
        for r in range(2):
            for copy in load(i, r):
                copy.wait()
            part = jnp.dot(nbuf[2 * i + r], wbuf[i, r], preferred_element_type=F32)
            out = part if out is None else out + part
        acc[...] += out
        return carry

    lax.fori_loop(0, 4, step, 0)
    own_ref[...] = acc[:512].T
    other_ref[...] = acc[512:].T


def kv_project(near, far, pieces):
    parts, rows, width = near.shape
    return pl.pallas_call(
        kv_kernel,
        in_specs=[HBM] * 6,
        out_specs=[full((128, rows))] * 2,
        out_shape=[jax.ShapeDtypeStruct((128, rows), F32)] * 2,
        scratch_shapes=[
            pltpu.VMEM((parts, 2 * rows, width), BF),
            pltpu.VMEM((4, 2, 512, 128), BF),
            pltpu.VMEM((2 * rows, 128), F32),
            pltpu.SemaphoreType.DMA((2, 8)),
            pltpu.SemaphoreType.DMA((4,)),
        ],
        compiler_params=pltpu.CompilerParams(vmem_limit_bytes=VMEM_MOST),
        cost_estimate=SIX_US,
        name="kv_project",
    )(near, far, *pieces)


def kv_finish_kernel(one_ref, two_ref, bias_ref, cos_ref, sin_ref, o_ref):
    kv = one_ref[...] + two_ref[...] + bias_ref[:, :1]
    first, second = kv[:64], kv[64:]
    cos, sin = cos_ref[...], sin_ref[...]
    o_ref[0:64] = (first * cos - second * sin).astype(BF)
    o_ref[64:128] = (second * cos + first * sin).astype(BF)


def kv_finish(one, two, bias, cos, sin):
    inputs = [one, two, bias, cos, sin]
    return pl.pallas_call(
        kv_finish_kernel,
        in_specs=[full(v.shape) for v in inputs],
        out_specs=full(one.shape),
        out_shape=jax.ShapeDtypeStruct(one.shape, BF),
        compiler_params=pltpu.CompilerParams(vmem_limit_bytes=8 << 20),
        cost_estimate=CHEAP,
        name="kv_finish",
    )(*inputs)


def q_kernel(first, near_ref, far_ref, *refs):
    w_refs, refs = refs[:4], refs[4:]
    so_far, refs = refs[:-9], refs[-9:]
    own_ref, other_ref, nbuf, wbuf, acc, nsem, wsem, before, bsem = refs
    rows = own_ref.shape[0]
    load = lambda k: tokens((near_ref, far_ref), first + k, nbuf, nsem, k)
    for k, w_ref in enumerate(w_refs):
        pltpu.make_async_copy(w_ref, wbuf.at[k], wsem.at[k]).start()
        if k < 2:
            for copy in load(k):
                copy.start()

    earlier = [pltpu.make_async_copy(ref, before.at[t], bsem.at[t]) for t, ref in enumerate(so_far)]
    for copy in earlier:
        copy.start()

    def part(i):
        out = None
        for r in range(2):
            k = 2 * i + r
            if k < 2:
                for copy in load(k + 2):
                    copy.start()
            pltpu.make_async_copy(w_refs[0], wbuf.at[k], wsem.at[k]).wait()
            for copy in load(k):
                copy.wait()
            one = jnp.dot(nbuf[k], wbuf[k], preferred_element_type=F32)
            out = one if out is None else out + one
        return out

    acc[...] = part(0)
    total = acc[...] + part(1)
    for copy in earlier:
        copy.wait()
    for t, o_ref in ((0, own_ref), (1, other_ref)):
        half = total[t * rows : (t + 1) * rows]
        o_ref[...] = half + before[t] if so_far else half


def q_project(first, near, far, pieces, so_far):
    parts, rows, width = near.shape
    shape = jax.ShapeDtypeStruct((rows, 256), F32)
    return pl.pallas_call(
        functools.partial(q_kernel, first),
        in_specs=[HBM] * (6 + len(so_far)),
        out_specs=[full(shape.shape)] * 2,
        out_shape=[shape] * 2,
        scratch_shapes=[
            pltpu.VMEM((4, 2 * rows, width), BF),
            pltpu.VMEM((4, 512, 256), BF),
            pltpu.VMEM((2 * rows, 256), F32),
            pltpu.SemaphoreType.DMA((2, 4)),
            pltpu.SemaphoreType.DMA((4,)),
            pltpu.VMEM((2, rows, 256), F32),
            pltpu.SemaphoreType.DMA((2,)),
        ],
        compiler_params=pltpu.CompilerParams(vmem_limit_bytes=VMEM_MOST),
        cost_estimate=THREE_US,
        name="q_project",
    )(near, far, *pieces, *so_far)


def choose_kernel(row_tab, col_tab, *refs):
    sources, outs = refs[:4], refs[4:]
    for f in range(4):
        for e in range(4):

            @pl.when(row_tab[f] == e)
            def _():
                outs[f][...] = sources[e][col_tab[f]]


def choose(row_tab, col_tab, sources):
    shape = sources[0].shape
    return pl.pallas_call(
        choose_kernel,
        grid_spec=pltpu.PrefetchScalarGridSpec(
            num_scalar_prefetch=2,
            grid=(1,),
            in_specs=[full(shape)] * 4,
            out_specs=[full(shape[1:])] * 4,
        ),
        out_shape=[jax.ShapeDtypeStruct(shape[1:], BF)] * 4,
        compiler_params=pltpu.CompilerParams(vmem_limit_bytes=8 << 20),
        cost_estimate=CHEAP,
        name="choose",
    )(row_tab, col_tab, *sources)


def q_finish_kernel(order, one_ref, two_ref, bias_ref, cos_ref, sin_ref, *outs):
    for d, o_ref in enumerate(outs):
        rows = pl.ds(pl.multiple_of(order[d] * 128, 128), 128)
        for h in range(2):
            cols = slice(h * 128, (h + 1) * 128)
            u = one_ref[rows, cols] + two_ref[rows, cols] + bias_ref[0:1, cols].astype(F32)
            o_ref[:, cols] = (u * cos_ref[rows, :] + pltpu.roll(u, 64, 1) * sin_ref[rows, :]).astype(BF)


def q_finish(order, one, two, bias, cos, sin):
    inputs = [one, two, bias, cos, sin]
    return pl.pallas_call(
        q_finish_kernel,
        grid_spec=pltpu.PrefetchScalarGridSpec(
            num_scalar_prefetch=1,
            grid=(1,),
            in_specs=[full(v.shape) for v in inputs],
            out_specs=[full((128, 256))] * 4,
        ),
        out_shape=[jax.ShapeDtypeStruct((128, 256), BF)] * 4,
        compiler_params=pltpu.CompilerParams(vmem_limit_bytes=8 << 20),
        cost_estimate=CHEAP,
        name="q_finish",
    )(order, *inputs)


def assemble_kernel(tab, *refs):
    o_ref = refs[4]
    for a in range(4):
        col = pl.multiple_of(tab[8 + a] * 512, 512)
        for i in range(2):
            o_ref[i, :, pl.ds(col, 512)] = refs[a][tab[5] ^ i]


def assemble(tab, base):
    shape = jax.ShapeDtypeStruct((2, 128, 2048), BF)
    return pl.pallas_call(
        assemble_kernel,
        grid_spec=pltpu.PrefetchScalarGridSpec(
            num_scalar_prefetch=1,
            grid=(1,),
            in_specs=[full(a.shape) for a in base],
            out_specs=full(shape.shape),
        ),
        out_shape=shape,
        compiler_params=pltpu.CompilerParams(vmem_limit_bytes=8 << 20),
        cost_estimate=CHEAP,
        name="assemble",
    )(tab, *base)


def attention_kernel(tab, q0, q1, q2, q3, own_ref, near_ref, far_ref, o_ref, qs, kv, sems):
    core, value_side = tab[4], tab[5]
    copies = [
        pltpu.make_async_copy(ref, kv.at[place_at], sems.at[i])
        for i, (ref, place_at) in enumerate(((near_ref, core), (far_ref, 1 - core)))
    ]
    for copy in copies:
        copy.start()
    own_kt = own_ref.at[value_side]
    own_vt = own_ref.at[value_side ^ 1]
    for f, q_ref in enumerate((q0, q1, q2, q3)):
        where = tab[12 + f]
        off = pl.multiple_of(lax.rem(where, 2) * 128, 128)
        for h in range(2):
            qs[where // 2, pl.ds(h * 256 + off, 128), :] = q_ref[:, h * 128 : (h + 1) * 128]

    factor = (128 ** -0.5) * math.log2(math.e)

    def lanes(p):
        total = p[:, :128]
        for i in range(1, p.shape[1] // 128):
            total = total + p[:, i * 128 : (i + 1) * 128]
        return total

    def pv(p, v):
        return lax.dot_general(p.astype(BF), v, (((1,), (1,)), ((), ())), preferred_element_type=F32)

    def first(blk):
        live = tab[2 + blk]
        c0 = blk * 256
        s = jnp.dot(qs[blk], own_kt[:, c0 : c0 + 256], preferred_element_type=F32) * factor
        row = lax.broadcasted_iota(jnp.int32, (512, 256), 0)
        row = jnp.where(row >= 256, row - 256, row)
        column = lax.broadcasted_iota(jnp.int32, (512, 256), 1)
        mask = (column <= row) & (column < live)
        s = jnp.where(mask, s, -1e30)
        top = jnp.max(s, axis=1, keepdims=True)
        p = jnp.where(mask, jnp.exp2(s - top), 0.0)
        return (top, lanes(p), pv(p, own_vt[:, c0 : c0 + 256]))

    def wide(blk, i, state):
        top, total, acc = state
        keys = pl.ds(pl.multiple_of(i * 512, 512), 512)
        ss = [jnp.dot(qs[blk], kv[side, 0, :, keys], preferred_element_type=F32) * factor for side in range(2)]
        new = jnp.maximum(top, jnp.max(jnp.maximum(ss[0], ss[1]), axis=1, keepdims=True))
        ps = [jnp.exp2(s - new) for s in ss]
        decay = jnp.exp2(top - new)
        total = total * decay + (lanes(ps[0]) + lanes(ps[1]))
        return (new, total, acc * decay + (pv(ps[0], kv[0, 1, :, keys]) + pv(ps[1], kv[1, 1, :, keys])))

    def step(blk, c, width, state):
        top, total, acc = state
        side = lax.rem(c, 2)
        keys = pl.ds(pl.multiple_of(c // 2 * 512, 512), width)
        s = jnp.dot(qs[blk], kv[side, 0, :, keys], preferred_element_type=F32) * factor
        new = jnp.maximum(top, jnp.max(s, axis=1, keepdims=True))
        p = jnp.exp2(s - new)
        decay = jnp.exp2(top - new)
        return (new, total * decay + lanes(p), acc * decay + pv(p, kv[side, 1, :, keys]))

    states = [first(0), first(1)]
    for copy in copies:
        copy.wait()
    for blk in range(2):
        n = tab[blk]
        state = lax.fori_loop(0, n // 4, lambda i, st: wide(blk, i, st), states[blk])
        state = lax.fori_loop(n // 4 * 2, n // 2, lambda c, st: step(blk, c, 512, st), state)
        state = lax.fori_loop(0, lax.rem(n, 2), lambda i, st: step(blk, n // 2, 256, st), state)
        top, total, acc = state
        result = (acc / jnp.sum(total, axis=1, keepdims=True)).astype(BF)
        for h in range(2):
            o_ref[blk * 256 : (blk + 1) * 256, h * 128 : (h + 1) * 128] = result[h * 256 : (h + 1) * 256]


def attention(tab, candidates, own, near, far):
    inputs = [*candidates, own]
    return pl.pallas_call(
        attention_kernel,
        grid_spec=pltpu.PrefetchScalarGridSpec(
            num_scalar_prefetch=1,
            grid=(1,),
            in_specs=[full(a.shape) for a in inputs] + [HBM] * 2,
            out_specs=full((512, 256)),
            scratch_shapes=[
                pltpu.VMEM((2, 512, 128), BF),
                pltpu.VMEM((2, 2, 128, 2048), BF),
                pltpu.SemaphoreType.DMA((2,)),
            ],
        ),
        out_shape=jax.ShapeDtypeStruct((512, 256), BF),
        compiler_params=pltpu.CompilerParams(vmem_limit_bytes=VMEM_LIMIT),
        cost_estimate=CHEAP,
        name="attention",
    )(tab, *inputs, near, far)


def shift(v, axis, by):
    n = lax.axis_size(axis)
    return lax.ppermute(v, axis, [(i, (i + by) % n) for i in range(n)])


def flip(v, axis, bits):
    n = lax.axis_size(axis)
    return lax.ppermute(v, axis, [(i, i ^ bits) for i in range(n)])


def after(value, *others):
    return lax.optimization_barrier((value, *others))[0]


def each(fn, values, *others):
    return [fn(after(v, *others) if others else v) for v in values]


def local(
    hidden,
    norm_gain,
    trainer_query,
    trainer_query_bias,
    trainer_kv,
    trainer_kv_bias,
    matching,
    block_lists,
    completion_lengths,
):
    zh, x, core, y, zl = (lax.axis_index(a).astype(jnp.int32) for a in (ZH, X, CORE, Y, ZL))
    rows = hidden.shape[0]
    ctx = (zh * 4 + x) * 2 + core
    four = jnp.arange(4, dtype=jnp.int32)

    ks = jnp.arange(16, dtype=jnp.int32)
    order = ((zh ^ ((ks >> 2) & 1)) * 4 + (x ^ (ks & 3))) * 2 + (core ^ (ks >> 3))
    near, far_out = norm(hidden, norm_gain, order)

    value_side = zl & 1
    half_at = lambda v: lax.dynamic_slice_in_dim(
        lax.dynamic_index_in_dim(v, y, 0, keepdims=False), value_side * 128, 128, v.ndim - 2
    )
    packed = half_at(trainer_kv)
    own_bias = jnp.broadcast_to(half_at(trainer_kv_bias).astype(F32)[:, None], (128, 128))

    s0 = trainer_query[0]
    z0 = flip(s0, ZH, 1)
    both = jnp.stack([packed, flip(packed, ZH, 1)])
    s_near = [s0] + [flip(s0, X, d) for d in (1, 2, 3)]
    near, far_out, z0, both, *s_near = lax.optimization_barrier((near, far_out, z0, both, *s_near))
    far = flip(far_out, CORE, 1)
    p_near = [both] + [flip(both, X, d) for d in (1, 2, 3)]
    z0 = after(z0, p_near[1])
    z_near = [z0] + [flip(z0, X, d) for d in (1, 2, 3)]

    q_half = list(q_project(0, near, far, s_near, []))
    kv_own, kv_other = kv_project(after(near, q_half[0]), far, p_near)
    counts = jnp.sum((after(block_lists, kv_own) >= 0).astype(jnp.int32), axis=1)
    token = jnp.arange(rows, dtype=jnp.int32)
    positions = (jnp.where(token < BLK, counts[0], counts[1]) - 1) * BLK + token % BLK
    freqs = THETA ** (-2.0 * jnp.arange(64, dtype=F32) / 128)
    angles = positions.astype(F32)[:, None] * freqs[None, :]
    cosine, sine = jnp.cos(angles), jnp.sin(angles)
    cos2 = jnp.concatenate([cosine, cosine], axis=1)
    sin2 = jnp.concatenate([-sine, sine], axis=1)
    cos_t = jnp.where(value_side == 0, cosine.T, 1.0)
    sin_t = jnp.where(value_side == 0, sine.T, 0.0)

    kv_other, q_half[0], cos_t, sin_t, cos2, sin2, *z_near = lax.optimization_barrier(
        (kv_other, q_half[0], cos_t, sin_t, cos2, sin2, *z_near)
    )
    piece = kv_finish(kv_own, flip(kv_other, CORE, 1), own_bias, cos_t, sin_t)
    over = flip(piece, ZH, 1)
    start = jnp.where(zh == 0, piece, over)
    pair = jnp.stack([start, piece])
    mate = flip(pair, ZL, 1)
    base0 = jnp.stack([pair[0], mate[0]])
    own = jnp.stack([pair[1], mate[1]])

    q_own, q_other = q_project(4, near, far, z_near, q_half)
    parts = q_finish(zl ^ four, q_own, flip(q_other, CORE, 1), trainer_query_bias, cos2, sin2)
    mine = jnp.stack([parts[0]] + [flip(parts[d], ZL, d) for d in (1, 2, 3)])
    mine, base0 = lax.optimization_barrier((mine, base0))
    gathered = [mine] + [flip(mine, Y, e) for e in (1, 2, 3)]
    base_near = [base0] + [flip(base0, X, d) for d in (1, 2, 3)]
    target = y * 4 + (zl ^ four)
    src = jnp.sum(
        jnp.where(matching[None, :] == target[:, None], jnp.arange(16, dtype=jnp.int32)[None, :], 0), axis=1
    )
    tab_1 = ((src // 4) ^ y).astype(jnp.int32)
    tab_1, *base_near = lax.optimization_barrier((tab_1, *base_near))
    sent = choose(tab_1, ((src % 4) ^ zl).astype(jnp.int32), gathered)
    base_near[0] = after(base_near[0], sent[0])
    candidates = [sent[0]] + [flip(sent[f], ZL, f) for f in (1, 2, 3)]

    blocks = ctx * 2 + jnp.arange(2, dtype=jnp.int32)
    slots = jnp.arange(16, dtype=jnp.int32)
    lengths = jnp.sum(
        jnp.where((blocks[:, None] - 16) == slots[None, :], completion_lengths[None, :], 0), axis=1
    )
    live = jnp.where(blocks < 16, BLK, lengths)
    tab = jnp.concatenate(
        [
            counts - 1,
            live,
            core[None],
            value_side[None],
            jnp.zeros((2,), jnp.int32),
            x ^ four,
            zl ^ four,
        ]
    ).astype(jnp.int32)
    whole = assemble(tab, base_near)
    return attention(tab, candidates, own, whole, flip(whole, CORE, 1))


def solution(mesh):
    fine = Mesh(mesh.devices.reshape(2, 4, 2, 4, 4), (ZH, X, CORE, Y, ZL))
    ctx = (ZH, X, CORE)
    tp = (Y, ZL)
    in_specs = (
        P(ctx, None),
        P(),
        P(tp, ctx, None),
        P(tp, None),
        P(None, ctx, None),
        P(),
        P(),
        P(ctx, None),
        P(),
    )
    return jax.shard_map(local, mesh=fine, in_specs=in_specs, out_specs=P(ctx, tp), check_vma=False)
```
